32 devices in a mesh: patch: 2 (over y), sky: 4 (over z), exp: 2 (over core), band: 2 (over x).
Axes of the slice: x: 2, y: 2, z: 4, core: 2. Of those that a mesh axis runs over, the one named last changes fastest.
Arguments:
- images: bfloat16 [2, 20, 1024, 512], P('band', 'exp', ('patch', 'sky')), parts along dimension 2, may hold values from -400 to 400
- valid_mask: int32 [2, 20, 1024, 512], P('band', 'exp', ('patch', 'sky')), parts along dimension 2, may hold values from 0 to 1, as said below
- row_kernel: float32 [2, 20, 31], P('band', 'exp'), may hold values from 0.01 to 0.06
- col_kernel: float32 [2, 20, 31], P('band', 'exp'), may hold values from 0.01 to 0.06
- exp_group: int32 [2, 20], P('band', 'exp'), may hold values from 0 to 15
- zero_point: float32 [2, 16], P('band'), may hold values from 0.5 to 2
- psf_row: float32 [2, 31], P('band'), may hold values from 0.01 to 0.06
- psf_col: float32 [2, 31], P('band'), may hold values from 0.01 to 0.06
Outputs:
- coadd_image: float32 [2, 1024, 512], P('band', ('patch', 'sky')), parts along dimension 1
- detection: float32 [1024, 512], P(('patch', 'sky'), 'band'), parts along dimension 0
The draws below stay inside these ranges and needn't reach their ends.
There are 2 independent parts, one for each index of `patch`. The reference program is written for one: setup_inputs(seed, part) draws one part's arguments, and reference() takes and returns one part's arrays. A program takes and returns all parts, laid end to end along the dimension named above; an argument that names none is the same for every part. Nothing has to cross between parts.
Inputs may be any that keep to these rules, and one draw needn't show every extreme that they name: For every band and pixel at least 10 of the 20 visits have valid_mask 1; exactly that many at some pixels, all of them at others.
All inputs are finite; a program needn't handle non-finite values.
Results may differ from the reference program's by a relative error of at most 0.0006.
Values may be sent and summed in bfloat16 or wider, within the bound.
No kernel may reach another device: no remote copies, remote signals or barrier semaphores. Data moves between devices by JAX's collectives and lax.ppermute only.
A program may use at most 64 MiB of HBM per device.

```python
import math
import jax
import jax.numpy as jnp
from jax import lax

COLS = 512
HALF = 15
REJECT = 4
GROUPS = 16
TAPS = 31
BANDS = 2
VIS_BAND = 20
ROWS = 512


def draw_images(key, part):
    key_noise, key_col, key_spike, key_sign = jax.random.split(key, 4)
    shape_all = (BANDS, VIS_BAND, ROWS, COLS)
    row_frac = jnp.arange(ROWS, dtype=jnp.float32) / max(ROWS - 1, 1)
    col_scale = 10.0 ** (jax.random.uniform(key_col, (COLS,), jnp.float32) - 0.5)
    jitter = jax.random.normal(key_noise, shape_all, jnp.float32)
    jitter = jnp.clip(jitter, -6.0, 6.0)
    row_scale = 10.0 ** (row_frac - 0.5)
    spike_on = (jax.random.randint(key_spike, shape_all, 0, 25) == 0).astype(jnp.float32)
    spike_sign = (jax.random.randint(key_sign, shape_all, 0, 2) * 2 - 1).astype(jnp.float32)
    sampled = (jitter + 12.0 * spike_on * spike_sign) * row_scale[:, None] * col_scale[None, :]
    return sampled.astype(jnp.bfloat16)


def draw_valid_mask(key, part):
    key_score, key_limit = jax.random.split(jax.random.fold_in(key, 7), 2)
    shape_all = (BANDS, VIS_BAND, ROWS, COLS)
    scores = jax.random.randint(key_score, shape_all, 0, 1 << 20) * VIS_BAND + jnp.arange(VIS_BAND, dtype=jnp.int32)[None, :, None, None]

    def count_below(visit_num, rank_count):
        picked = lax.dynamic_index_in_dim(scores, visit_num, 1, keepdims=True)
        return rank_count + (picked < scores).astype(jnp.int32)
    rank_count = lax.fori_loop(0, VIS_BAND, count_below, jnp.zeros(shape_all, jnp.int32))
    cutoff = jax.random.randint(key_limit, (BANDS, 1, ROWS, COLS), 2 * REJECT + 2, VIS_BAND + 1)
    return (rank_count < cutoff).astype(jnp.int32)


def touch_ends(drawn, key, low, largest):
    extent = drawn.shape
    index_at = [jax.random.randint(jax.random.fold_in(key, axis), (), 0, extent[axis]) for axis in range(len(extent))]
    drawn = drawn.at[tuple(index_at)].set(low)
    longest = extent.index(max(extent))
    index_at[longest] = (index_at[longest] + 1) % extent[longest]
    return drawn.at[tuple(index_at)].set(largest)


def steps_of(key, dims, pieces, smallest, high):
    factor_of, own = 1.0, jax.random.fold_in(key, 6)
    for dim, shards_of in pieces:
        heights = jnp.exp(jax.random.uniform(jax.random.fold_in(own, dim), (shards_of,), jnp.float32, smallest / len(pieces), high / len(pieces)))
        factor_of = factor_of * jnp.repeat(heights, dims[dim] // shards_of).reshape([-1 if axis == dim else 1 for axis in range(len(dims))])
    return factor_of


def setup_inputs(seed: int = 0, part: int = 0) -> dict:
    seeds = jax.random.split(jax.random.key(seed), 9)
    own_keys = jax.random.split(jax.random.fold_in(seeds[8], part), 9)
    images = draw_images(jax.random.fold_in(jax.random.fold_in(seeds[8], part), 71), part)
    valid_mask = draw_valid_mask(jax.random.fold_in(jax.random.fold_in(seeds[8], part), 71), part)
    row_kernel = jnp.clip(jnp.exp(math.log(0.06) - 1.7917595 * jax.random.uniform(seeds[2], (BANDS, VIS_BAND, TAPS), jnp.float32) ** steps_of(seeds[2], (BANDS, VIS_BAND, TAPS), ((0, 2), (1, 2)), -0.2, 0.2)), 0.01, 0.06)
    col_kernel = jnp.clip(jnp.exp(math.log(0.06) - 1.7917595 * jax.random.uniform(seeds[3], (BANDS, VIS_BAND, TAPS), jnp.float32) ** steps_of(seeds[3], (BANDS, VIS_BAND, TAPS), ((0, 2), (1, 2)), -0.2, 0.2)), 0.01, 0.06)
    exp_group = touch_ends(jax.random.randint(seeds[4], (BANDS, VIS_BAND), 0, GROUPS), jax.random.fold_in(seeds[4], 1), 0, GROUPS - 1).astype(jnp.int32)
    zero_point = jnp.clip(jnp.exp(math.log(2.0) - 1.3862944 * jax.random.uniform(seeds[5], (BANDS, GROUPS), jnp.float32) ** steps_of(seeds[5], (BANDS, GROUPS), ((0, 2),), -0.2, 0.2)), 0.5, 2.0)
    psf_row = jnp.clip(jnp.exp(math.log(0.06) - 1.7917595 * jax.random.uniform(seeds[6], (BANDS, TAPS), jnp.float32) ** steps_of(seeds[6], (BANDS, TAPS), ((0, 2),), -0.2, 0.2)), 0.01, 0.06)
    psf_col = jnp.clip(jnp.exp(math.log(0.06) - 1.7917595 * jax.random.uniform(seeds[7], (BANDS, TAPS), jnp.float32) ** steps_of(seeds[7], (BANDS, TAPS), ((0, 2),), -0.2, 0.2)), 0.01, 0.06)
    return dict(images=images, valid_mask=valid_mask, row_kernel=row_kernel, col_kernel=col_kernel, exp_group=exp_group, zero_point=zero_point, psf_row=psf_row, psf_col=psf_col)


SENTINEL = 1.0e30
EPSILON = 1.0e-5


def rows_filter(padded, kernel, height):
    result = kernel[..., 0][..., None, None] * padded[..., 0:height, :]
    for offset in range(1, TAPS):
        result = result + kernel[..., offset][..., None, None] * padded[..., offset:offset + height, :]
    return result


def cols_filter(grid_in, kernel):
    columns = grid_in.shape[-1]
    widths = [(0, 0)] * (grid_in.ndim - 1) + [(HALF, HALF)]
    padded = jnp.pad(grid_in, widths)
    result = kernel[..., 0][..., None, None] * padded[..., 0:columns]
    for offset in range(1, TAPS):
        result = result + kernel[..., offset][..., None, None] * padded[..., offset:offset + columns]
    return result


def one_band(inputs):
    band_images, band_valid, band_rows, band_cols, band_groups, band_points = inputs
    padded = jnp.pad(band_images.astype(jnp.float32), ((0, 0), (HALF, HALF), (0, 0)))
    smeared = cols_filter(rows_filter(padded, band_rows, ROWS), band_cols)
    matches = band_groups[:, None] == jnp.arange(GROUPS, dtype=jnp.int32)[None, :]
    flux_scale = jnp.sum(jnp.where(matches, band_points[None, :], jnp.float32(0.0)), axis=1)
    scaled_visits = flux_scale[:, None, None] * smeared
    usable = band_valid == 1
    upper_sum = jnp.sum(jnp.sort(jnp.where(usable, scaled_visits, -SENTINEL), axis=0)[VIS_BAND - REJECT:], axis=0)
    lower_sum = jnp.sum(jnp.sort(jnp.where(usable, scaled_visits, SENTINEL), axis=0)[:REJECT], axis=0)
    flux_sum = jnp.sum(jnp.where(usable, scaled_visits, jnp.float32(0.0)), axis=0)
    valid_count = jnp.sum(usable.astype(jnp.float32), axis=0)
    return (flux_sum - upper_sum - lower_sum) / (valid_count - 2 * REJECT)


def reference(images, valid_mask, row_kernel, col_kernel, exp_group, zero_point, psf_row, psf_col):
    coadd_image = lax.map(one_band, (images, valid_mask, row_kernel, col_kernel, exp_group, zero_point))
    padded = jnp.pad(coadd_image, ((0, 0), (HALF, HALF), (0, 0)))
    filtered = cols_filter(rows_filter(padded, psf_row, ROWS), psf_col)
    energy = filtered * filtered
    variance = jnp.sum(energy, axis=(1, 2)) / (ROWS * COLS) + EPSILON
    detection = jnp.sum(energy / variance[:, None, None], axis=0)
    return (coadd_image, detection)
```

```python
import functools

import jax
import jax.numpy as jnp
from jax import lax
from jax.experimental import pallas as pl
from jax.experimental.pallas import tpu as pltpu
from jax.sharding import PartitionSpec as P

HALF = 15
REJECT = 4
TAPS = 31
EDGE = 16
LANES = 128
SENTINEL = 1e30
EPSILON = 1e-05
F32 = jnp.float32
BF16 = jnp.bfloat16
MIB = 1024 * 1024


def split2(value):
    high = value.astype(BF16)
    return high, (value - high.astype(F32)).astype(BF16)


def band_rows(taps, rows):
    return pltpu.roll(
        jnp.broadcast_to(pltpu.roll(taps, 1, 1), (rows, LANES)), 0, 1, stride=1, stride_axis=0
    )


def square_masks():
    row = lax.broadcasted_iota(jnp.int32, (LANES, LANES), 0)
    col = lax.broadcasted_iota(jnp.int32, (LANES, LANES), 1)
    return row, col


def col_matrix(taps):
    square = band_rows(taps, LANES).T
    row, col = square_masks()
    whole = jnp.concatenate(
        [jnp.where(row > col, square, 0.0), jnp.where(row < col, square, 0.0)], axis=0
    )
    return jnp.concatenate(split2(whole), axis=1)


def row_matrix(taps):
    square = band_rows(taps, LANES)
    row, col = square_masks()
    return jnp.concatenate(
        [jnp.where(col > row, square, 0.0), jnp.where(col < row, square, 0.0)], axis=1
    )


def col_conv(value, matrix):
    rows, cols = value.shape
    tiles = cols // LANES
    turned = pltpu.roll(value, EDGE, 1)
    first = turned[:, :LANES]
    lane = lax.broadcasted_iota(jnp.int32, (rows, LANES), 1)
    wide = jnp.concatenate(
        [jnp.where(lane < EDGE, 0.0, first), turned[:, LANES:], jnp.where(lane < EDGE, first, 0.0)],
        axis=1,
    )
    parts = [
        part[:, n * LANES : (n + 2) * LANES] for part in split2(wide) for n in range(tiles)
    ]
    product = jnp.dot(jnp.concatenate(parts, axis=0), matrix, preferred_element_type=F32)

    def piece(n, side):
        return product[n * rows : (n + 1) * rows, side * LANES : (side + 1) * LANES]

    return jnp.concatenate(
        [piece(n, 0) + (piece(n, 1) + piece(tiles + n, 0)) for n in range(tiles)], axis=1
    )


def exchange(values, i, j):
    values[i], values[j] = (
        jnp.maximum(values[i], values[j]),
        jnp.minimum(values[i], values[j]),
    )


def cleaned(values):
    for i, j in ((0, 2), (1, 3), (0, 1), (2, 3)):
        exchange(values, i, j)
    return values


def top_sorted(values):
    best = None
    for start in range(0, len(values), REJECT):
        group = list(values[start : start + REJECT])
        if len(group) == 4:
            for i, j in ((0, 1), (2, 3), (0, 2), (1, 3), (1, 2)):
                exchange(group, i, j)
        elif len(group) == 3:
            for i, j in ((0, 1), (1, 2), (0, 1)):
                exchange(group, i, j)
        elif len(group) == 2:
            exchange(group, 0, 1)
        if best is None:
            best = group
        else:
            for i, value in enumerate(group):
                best[REJECT - 1 - i] = jnp.maximum(best[REJECT - 1 - i], value)
            best = cleaned(best)
    return best


def sort_visits(values, lists):
    visits, rows, cols = values.shape
    width = 2 * LANES

    def body(step, carry):
        at = pl.ds(pl.multiple_of(step * 8, 8), 8)
        for start in range(0, cols, width):
            lanes = pl.ds(start, width)
            low = [values[v, at, lanes] for v in range(visits)]
            dead = [value == SENTINEL for value in low]
            upper = top_sorted([jnp.where(d, -SENTINEL, v) for d, v in zip(dead, low)])
            total, count = 0.0, 0.0
            for d, v in zip(dead, low):
                total = total + jnp.where(d, 0.0, v)
                count = count + jnp.where(d, 0.0, 1.0)
            lower = top_sorted([-v for v in low])
            for i in range(REJECT):
                lists[i, at, lanes] = upper[i]
                lists[REJECT + i, at, lanes] = lower[i]
            lists[2 * REJECT, at, lanes] = total
            lists[2 * REJECT + 1, at, lanes] = count
        return carry

    lax.fori_loop(0, rows // 8, body, 0)


def inner_kernel(
    groups, points, images, mask, row_taps, col_taps, lists, row_out, col_out, taps, values
):
    visit = pl.program_id(0)
    visits = pl.num_programs(0)
    rows = lists.shape[1]

    @pl.when(visit == 0)
    def _():
        taps[...] = jnp.zeros_like(taps)
        taps[0, 0 : row_taps.shape[1], 0:TAPS] = row_taps[0]
        taps[1, 0 : col_taps.shape[1], 0:TAPS] = col_taps[0]

    scale = points[0, groups[0, visit]]
    row_m = jnp.concatenate(split2(band_rows(taps[0, pl.ds(visit, 1), :], rows)), axis=0)
    col_m = col_matrix(taps[1, pl.ds(visit, 1), :] * scale)
    row_out[0] = row_m
    col_out[0] = col_m
    both = jnp.dot(row_m, images[0, 0], preferred_element_type=F32)
    result = col_conv(both[:rows] + both[rows:], col_m)
    usable = mask[0, 0, pl.ds(EDGE, rows), :] == 1
    values[visit] = jnp.where(usable, result, SENTINEL)

    @pl.when(visit == visits - 1)
    def _():
        sort_visits(values, lists)


def edge_kernel(
    above, below, first, last, first_mask, last_mask, row_m, col_m, lists, values
):
    visits = values.shape[0]
    inner = row_m.shape[1] // 2
    cols = values.shape[2]
    reach = 3 * EDGE
    for visit in range(visits):
        pieces = []
        for start in (0, inner):
            pieces += [row_m[visit, start : start + EDGE], row_m[visit, start + reach : start + reach + EDGE]]
        window = jnp.concatenate(
            [
                above[visit],
                first[0, visit],
                last[0, visit],
                below[visit],
                jnp.zeros((LANES - 2 * reach, cols), BF16),
            ],
            axis=0,
        )
        both = jnp.dot(jnp.concatenate(pieces, axis=0), window, preferred_element_type=F32)
        result = col_conv(both[: 2 * EDGE] + both[2 * EDGE :], col_m[visit])
        usable = jnp.concatenate([first_mask[0, visit], last_mask[0, visit]], axis=0) == 1
        values[visit] = jnp.where(usable, result, SENTINEL)
    sort_visits(values, lists)


def merge_kernel(mine, other, coadd):
    def body(step, carry):
        at = pl.ds(pl.multiple_of(step * 8, 8), 8)
        upper, lower = 0.0, 0.0
        for i in range(REJECT):
            j = REJECT - 1 - i
            upper = upper + jnp.maximum(mine[i, at, :], other[j, at, :])
            lower = lower + jnp.maximum(mine[REJECT + i, at, :], other[REJECT + j, at, :])
        total = mine[2 * REJECT, at, :] + other[2 * REJECT, at, :]
        count = mine[2 * REJECT + 1, at, :] + other[2 * REJECT + 1, at, :]
        coadd[at, :] = (total - upper + lower) / (count - 2 * REJECT)
        return carry

    lax.fori_loop(0, coadd.shape[0] // 8, body, 0)


def psf_kernel(place, above, below, edges, inner, row_taps, col_taps, coadd, pieces, taps):
    height, cols = coadd.shape[1:]
    bands, _, width = pieces.shape
    coadd[0, 0:EDGE] = edges[0:EDGE]
    coadd[0, EDGE : height - EDGE] = inner[...]
    coadd[0, height - EDGE : height] = edges[EDGE : 2 * EDGE]
    taps[...] = jnp.zeros_like(taps)
    taps[0:1, 0:TAPS] = row_taps[...]
    taps[8:9, 0:TAPS] = col_taps[...]
    row_h, row_l = split2(row_matrix(taps[0:1, :]))
    col_m = col_matrix(taps[8:9, :])
    mid_h, mid_l = split2(coadd[0])
    rest = jnp.zeros((2 * LANES - height - 2 * EDGE, cols), BF16)
    empty = jnp.zeros((EDGE, cols), BF16)
    high = jnp.concatenate([above[...], mid_h, below[...], rest], axis=0)
    low = jnp.concatenate([empty, mid_l, empty, rest], axis=0)
    both = jnp.dot(jnp.concatenate([row_h, row_l], axis=0), high, preferred_element_type=F32)
    both_low = jnp.dot(row_h, low, preferred_element_type=F32)
    filtered = col_conv(both[:height] + (both[height:] + both_low), col_m)
    energy = filtered * filtered
    part = jnp.sum(energy.reshape(height // 8, 8, cols), axis=0)
    part = sum(part[:, n * LANES : (n + 1) * LANES] for n in range(cols // LANES))
    own = place[0]
    for band in range(bands):
        slot = lax.rem(band - own + bands, bands)
        pieces[slot, 0:height, :] = energy[:, band * width : (band + 1) * width]
    for slot in range(bands):
        pieces[slot, height : height + 8, :] = jnp.concatenate([part] * (width // LANES), axis=1)


def final_kernel(pixels, pieces, sums, detection):
    height = detection.shape[0]
    total = 0.0
    for i in range(len(pieces)):
        variance = jnp.sum(sums[i, :, :]) / pixels + EPSILON
        total = total + pieces[i][...] / variance
    detection[...] = total


def vmem(shape, dtype=F32):
    return jax.ShapeDtypeStruct(shape, dtype)


VMEM = pl.BlockSpec(memory_space=pltpu.VMEM)
SMEM = pl.BlockSpec(memory_space=pltpu.SMEM)
PARAMS = pltpu.CompilerParams(vmem_limit_bytes=40 * MIB)


def shifted(value, axis, step):
    size = lax.axis_size(axis)
    pairs = [(i, i + step) for i in range(size) if 0 <= i + step < size]
    return lax.ppermute(value, axis, pairs)


def turned(value, axis, step):
    size = lax.axis_size(axis)
    return lax.ppermute(value, axis, [(i, (i + step) % size) for i in range(size)])


def on_device(images, valid_mask, row_kernel, col_kernel, exp_group, zero_point, psf_row, psf_col):
    _, visits, height, cols = images.shape
    inner = height - 2 * EDGE
    bands = lax.axis_size("band")
    strips = lax.axis_size("sky")
    above = shifted(images[0, :, height - EDGE :, :], "sky", 1)
    below = shifted(images[0, :, :EDGE, :], "sky", -1)

    inner_lists, row_m, col_m = pl.pallas_call(
        inner_kernel,
        grid=(visits,),
        in_specs=[
            SMEM,
            SMEM,
            pl.BlockSpec((1, 1, height, cols), lambda v: (0, v, 0, 0)),
            pl.BlockSpec((1, 1, height, cols), lambda v: (0, v, 0, 0)),
            pl.BlockSpec((1, visits, TAPS), lambda v: (0, 0, 0)),
            pl.BlockSpec((1, visits, TAPS), lambda v: (0, 0, 0)),
        ],
        out_specs=[
            pl.BlockSpec((2 * REJECT + 2, inner, cols), lambda v: (0, 0, 0)),
            pl.BlockSpec((1, 2 * inner, LANES), lambda v: (v, 0, 0)),
            pl.BlockSpec((1, 2 * LANES, 2 * LANES), lambda v: (v, 0, 0)),
        ],
        out_shape=[
            vmem((2 * REJECT + 2, inner, cols)),
            vmem((visits, 2 * inner, LANES), BF16),
            vmem((visits, 2 * LANES, 2 * LANES), BF16),
        ],
        scratch_shapes=[
            pltpu.VMEM((2, -(-visits // 8) * 8, LANES), F32),
            pltpu.VMEM((visits, inner, cols), F32),
        ],
        compiler_params=PARAMS,
        name="inner_visits",
    )(exp_group, zero_point, images, valid_mask, row_kernel, col_kernel)
    swap = [(0, 1), (1, 0)]
    inner_other = lax.ppermute(inner_lists, "exp", swap)

    last_block = height // (2 * EDGE) - 1
    last_mask_block = height // EDGE - 1
    edge_lists = pl.pallas_call(
        edge_kernel,
        grid=(1,),
        in_specs=[
            pl.BlockSpec((visits, EDGE, cols), lambda i: (0, 0, 0)),
            pl.BlockSpec((visits, EDGE, cols), lambda i: (0, 0, 0)),
            pl.BlockSpec((1, visits, 2 * EDGE, cols), lambda i: (0, 0, 0, 0)),
            pl.BlockSpec((1, visits, 2 * EDGE, cols), lambda i: (0, 0, last_block, 0)),
            pl.BlockSpec((1, visits, EDGE, cols), lambda i: (0, 0, 0, 0)),
            pl.BlockSpec((1, visits, EDGE, cols), lambda i: (0, 0, last_mask_block, 0)),
            pl.BlockSpec((visits, 2 * inner, LANES), lambda i: (0, 0, 0)),
            pl.BlockSpec((visits, 2 * LANES, 2 * LANES), lambda i: (0, 0, 0)),
        ],
        out_specs=pl.BlockSpec((2 * REJECT + 2, 2 * EDGE, cols), lambda i: (0, 0, 0)),
        out_shape=vmem((2 * REJECT + 2, 2 * EDGE, cols)),
        scratch_shapes=[pltpu.VMEM((visits, 2 * EDGE, cols), F32)],
        compiler_params=PARAMS,
        name="edge_visits",
    )(above, below, images, images, valid_mask, valid_mask, row_m, col_m)
    edge_other = lax.ppermute(edge_lists, "exp", swap)

    def merged(mine, other):
        rows = mine.shape[1]
        return pl.pallas_call(
            merge_kernel,
            in_specs=[VMEM, VMEM],
            out_specs=VMEM,
            out_shape=vmem((rows, cols)),
            compiler_params=PARAMS,
            name="merge",
        )(mine, other)

    edges = merged(edge_lists, edge_other)
    coadd_above = shifted(edges[EDGE:].astype(BF16), "sky", 1)
    coadd_below = shifted(edges[:EDGE].astype(BF16), "sky", -1)
    inner_coadd = merged(inner_lists, inner_other)

    width = cols // bands
    place = lax.axis_index("band").astype(jnp.int32)[None]
    coadd_image, pieces = pl.pallas_call(
        psf_kernel,
        in_specs=[SMEM] + [VMEM] * 6,
        out_specs=[VMEM, VMEM],
        out_shape=[vmem((1, height, cols)), vmem((bands, height + 8, width))],
        scratch_shapes=[pltpu.VMEM((16, LANES), F32)],
        compiler_params=PARAMS,
        name="psf",
    )(place, coadd_above, coadd_below, edges, inner_coadd, psf_row, psf_col)

    parts = [pieces[0]] + [turned(pieces[k], "band", k) for k in range(1, bands)]
    sums = jnp.stack([part[height:, :LANES] for part in parts])
    if strips <= 4:
        sums = sum((turned(sums, "sky", k) for k in range(1, strips)), sums)
    else:
        sums = lax.psum(sums, "sky")
    pixels = height * strips * cols
    detection = pl.pallas_call(
        lambda *refs: final_kernel(pixels, refs[:bands], refs[bands], refs[bands + 1]),
        in_specs=[VMEM] * (bands + 1),
        out_specs=VMEM,
        out_shape=vmem((height, width)),
        compiler_params=PARAMS,
        name="detection",
    )(*[part[:height] for part in parts], sums)
    return coadd_image, detection


def solution(mesh):
    placed = (
        P("band", "exp", ("patch", "sky"), None),
        P("band", "exp", ("patch", "sky"), None),
        P("band", "exp", None),
        P("band", "exp", None),
        P("band", "exp"),
        P("band", None),
        P("band", None),
        P("band", None),
    )
    return jax.shard_map(
        on_device,
        mesh=mesh,
        in_specs=placed,
        out_specs=(P("band", ("patch", "sky"), None), P(("patch", "sky"), "band")),
        check_vma=False,
    )
```

```python
import functools

import jax
import jax.numpy as jnp
from jax import lax
from jax.experimental import pallas as pl
from jax.experimental.pallas import tpu as pltpu
from jax.sharding import PartitionSpec as P

HALF = 15
REJECT = 4
TAPS = 31
EDGE = 16
LANES = 128
SENTINEL = 1e30
EPSILON = 1e-05
F32 = jnp.float32
BF16 = jnp.bfloat16
MIB = 1024 * 1024
UNROLL = 2


def split2(value):
    high = value.astype(BF16)
    return high, (value - high.astype(F32)).astype(BF16)


def band_rows(taps, rows):
    return pltpu.roll(
        jnp.broadcast_to(pltpu.roll(taps, 1, 1), (rows, LANES)), 0, 1, stride=1, stride_axis=0
    )


def around_matrix(taps):
    base = pltpu.roll(taps, LANES - HALF, 1)
    return pltpu.roll(jnp.broadcast_to(base, (LANES, LANES)), 0, 1, stride=1, stride_axis=0)


def square_masks():
    row = lax.broadcasted_iota(jnp.int32, (LANES, LANES), 0)
    col = lax.broadcasted_iota(jnp.int32, (LANES, LANES), 1)
    return row, col


def col_matrix(taps):
    square = band_rows(taps, LANES).T
    row, col = square_masks()
    whole = jnp.concatenate(
        [jnp.where(row > col, square, 0.0), jnp.where(row < col, square, 0.0)], axis=0
    )
    return jnp.concatenate(split2(whole), axis=1)


def row_matrix(taps):
    square = band_rows(taps, LANES)
    row, col = square_masks()
    return jnp.concatenate(
        [jnp.where(col > row, square, 0.0), jnp.where(col < row, square, 0.0)], axis=1
    )


def col_conv(value, matrix):
    rows, cols = value.shape
    tiles = cols // LANES
    turned = pltpu.roll(value, EDGE, 1)
    first = turned[:, :LANES]
    lane = lax.broadcasted_iota(jnp.int32, (rows, LANES), 1)
    wide = jnp.concatenate(
        [jnp.where(lane < EDGE, 0.0, first), turned[:, LANES:], jnp.where(lane < EDGE, first, 0.0)],
        axis=1,
    )
    parts = [
        part[:, n * LANES : (n + 2) * LANES] for part in split2(wide) for n in range(tiles)
    ]
    product = jnp.dot(jnp.concatenate(parts, axis=0), matrix, preferred_element_type=F32)

    def piece(n, side):
        return product[n * rows : (n + 1) * rows, side * LANES : (side + 1) * LANES]

    return jnp.concatenate(
        [piece(n, 0) + (piece(n, 1) + piece(tiles + n, 0)) for n in range(tiles)], axis=1
    )


def exchange(values, i, j):
    values[i], values[j] = (
        jnp.maximum(values[i], values[j]),
        jnp.minimum(values[i], values[j]),
    )


def cleaned(values):
    for i, j in ((0, 2), (1, 3), (0, 1), (2, 3)):
        exchange(values, i, j)
    return values


def top_sorted(values):
    best = None
    for start in range(0, len(values), REJECT):
        group = list(values[start : start + REJECT])
        if len(group) == 4:
            for i, j in ((0, 1), (2, 3), (0, 2), (1, 3), (1, 2)):
                exchange(group, i, j)
        elif len(group) == 3:
            for i, j in ((0, 1), (1, 2), (0, 1)):
                exchange(group, i, j)
        elif len(group) == 2:
            exchange(group, 0, 1)
        if best is None:
            best = group
        else:
            for i, value in enumerate(group):
                best[REJECT - 1 - i] = jnp.maximum(best[REJECT - 1 - i], value)
            best = cleaned(best)
    return best


def sort_visits(values, lists):
    visits, rows, cols = values.shape
    width = 2 * LANES

    def body(step, carry):
        at = pl.ds(pl.multiple_of(step * 8, 8), 8)
        for start in range(0, cols, width):
            lanes = pl.ds(start, width)
            low = [values[v, at, lanes] for v in range(visits)]
            dead = [value == SENTINEL for value in low]
            upper = top_sorted([jnp.where(d, -SENTINEL, v) for d, v in zip(dead, low)])
            total, count = 0.0, 0.0
            for d, v in zip(dead, low):
                total = total + jnp.where(d, 0.0, v)
                count = count + jnp.where(d, 0.0, 1.0)
            lower = top_sorted([-v for v in low])
            for i in range(REJECT):
                lists[i, at, lanes] = upper[i]
                lists[REJECT + i, at, lanes] = lower[i]
            lists[2 * REJECT, at, lanes] = total
            lists[2 * REJECT + 1, at, lanes] = count
        return carry

    lax.fori_loop(0, rows // 8, body, 0)


def at_ends(above, below):
    strip = lax.axis_index("sky")
    top, bottom = strip == 0, strip == lax.axis_size("sky") - 1
    return (
        jnp.where(top, jnp.zeros_like(above), above),
        jnp.where(bottom, jnp.zeros_like(below), below),
    )


def inner_kernel(
    groups_h,
    points_h,
    images_h,
    mask_h,
    row_taps_h,
    col_taps_h,
    lists,
    part,
    edge_m,
    col_m,
    edge_mask,
    groups,
    points,
    row_taps,
    col_taps,
    images,
    mask,
    taps,
    row_m,
    values,
    small_sems,
    image_sems,
    mask_sems,
):
    visits, height, _ = images.shape
    small = [
        pltpu.make_async_copy(source, target, small_sems.at[i])
        for i, (source, target) in enumerate(
            ((groups_h, groups), (points_h, points), (row_taps_h, row_taps), (col_taps_h, col_taps))
        )
    ]

    def image_copy(v):
        return pltpu.make_async_copy(images_h.at[0, v], images.at[v], image_sems.at[v])

    def mask_copy(v):
        return pltpu.make_async_copy(mask_h.at[0, v], mask.at[v], mask_sems.at[v])

    for copy in small:
        copy.start()
    for v in range(visits):
        image_copy(v).start()
        mask_copy(v).start()
    taps[...] = jnp.zeros_like(taps)
    row, col = square_masks()
    near = jnp.abs(row - col) <= HALF
    for copy in small:
        copy.wait()
    def build(v, slot):
        taps[slot : slot + 1, 0:TAPS] = row_taps[v]
        taps[slot + 8 : slot + 9, 0:TAPS] = col_taps[v]
        scale = points[0, groups[0, v]]
        square = around_matrix(taps[slot : slot + 1, :])
        row_m[v] = jnp.concatenate(split2(jnp.where(near, square, 0.0)), axis=0)
        far = jnp.where(near, 0.0, square)
        far = jnp.concatenate([far[:EDGE], far[height - EDGE :]], axis=0)
        edge_m[v] = jnp.concatenate(split2(far), axis=0)
        col_m[v] = col_matrix(taps[slot + 8 : slot + 9, :] * scale)

    def convolve(v, slot):
        both = jnp.dot(row_m[v], images[v], preferred_element_type=F32)
        smeared = both[:height] + both[height:]
        part[v, 0:EDGE] = smeared[:EDGE]
        part[v, EDGE : 2 * EDGE] = smeared[height - EDGE :]
        result = col_conv(smeared[EDGE : height - EDGE], col_m[v])
        values[v] = jnp.where(mask[v, EDGE : height - EDGE] == 1, result, SENTINEL)
        edge_mask[v, 0:EDGE] = mask[v, 0:EDGE]
        edge_mask[v, EDGE : 2 * EDGE] = mask[v, height - EDGE :]

    def each(step_of, at_once):
        at_once = at_once if visits % at_once == 0 else 1

        def body(step, carry):
            for i in range(at_once):
                step_of(step * at_once + i, 16 * i)
            return carry

        lax.fori_loop(0, visits // at_once, body, 0)

    each(build, UNROLL)
    for v in range(visits):
        image_copy(v).wait()
        mask_copy(v).wait()
    each(convolve, UNROLL)
    sort_visits(values, lists)


def edge_kernel(above, below, part, edge_m, col_m, edge_mask, lists, values):
    visits, _, cols = values.shape
    for visit in range(visits):
        before, after = at_ends(above[visit], below[visit])
        window = jnp.concatenate(
            [after, jnp.zeros((LANES - 2 * EDGE, cols), BF16), before], axis=0
        )
        both = jnp.dot(edge_m[visit], window, preferred_element_type=F32)
        result = col_conv(part[visit] + (both[: 2 * EDGE] + both[2 * EDGE :]), col_m[visit])
        values[visit] = jnp.where(edge_mask[visit] == 1, result, SENTINEL)
    sort_visits(values, lists)


def merge_kernel(mine, other, coadd):
    def body(step, carry):
        at = pl.ds(pl.multiple_of(step * 8, 8), 8)
        upper, lower = 0.0, 0.0
        for i in range(REJECT):
            j = REJECT - 1 - i
            upper = upper + jnp.maximum(mine[i, at, :], other[j, at, :])
            lower = lower + jnp.maximum(mine[REJECT + i, at, :], other[REJECT + j, at, :])
        total = mine[2 * REJECT, at, :] + other[2 * REJECT, at, :]
        count = mine[2 * REJECT + 1, at, :] + other[2 * REJECT + 1, at, :]
        coadd[at, :] = (total - upper + lower) / (count - 2 * REJECT)
        return carry

    lax.fori_loop(0, coadd.shape[0] // 8, body, 0)


def psf_kernel(above, below, edges, inner, row_taps, col_taps, coadd, pieces, taps):
    height, cols = coadd.shape[1:]
    bands, _, width = pieces.shape
    coadd[0, 0:EDGE] = edges[0:EDGE]
    coadd[0, EDGE : height - EDGE] = inner[...]
    coadd[0, height - EDGE : height] = edges[EDGE : 2 * EDGE]
    taps[...] = jnp.zeros_like(taps)
    taps[0:1, 0:TAPS] = row_taps[...]
    taps[8:9, 0:TAPS] = col_taps[...]
    row_h, row_l = split2(row_matrix(taps[0:1, :]))
    col_m = col_matrix(taps[8:9, :])
    mid_h, mid_l = split2(coadd[0])
    rest = jnp.zeros((2 * LANES - height - 2 * EDGE, cols), BF16)
    empty = jnp.zeros((EDGE, cols), BF16)
    before, after = at_ends(above[...], below[...])
    high = jnp.concatenate([before, mid_h, after, rest], axis=0)
    low = jnp.concatenate([empty, mid_l, empty, rest], axis=0)
    both = jnp.dot(jnp.concatenate([row_h, row_l], axis=0), high, preferred_element_type=F32)
    both_low = jnp.dot(row_h, low, preferred_element_type=F32)
    filtered = col_conv(both[:height] + (both[height:] + both_low), col_m)
    energy = filtered * filtered
    part = jnp.sum(energy.reshape(height // 8, 8, cols), axis=0)
    part = sum(part[:, n * LANES : (n + 1) * LANES] for n in range(cols // LANES))
    own = lax.axis_index("band")
    for band in range(bands):
        slot = lax.rem(band - own + bands, bands)
        pieces[slot, 0:height, :] = energy[:, band * width : (band + 1) * width]
    for slot in range(bands):
        pieces[slot, height : height + 8, :] = jnp.concatenate([part] * (width // LANES), axis=1)


def final_kernel(pixels, pieces, sums, detection):
    height = detection.shape[0]
    total = 0.0
    for i in range(len(pieces)):
        variance = jnp.sum(sums[i, :, :]) / pixels + EPSILON
        total = total + pieces[i][...] / variance
    detection[...] = total


def vmem(shape, dtype=F32):
    return jax.ShapeDtypeStruct(shape, dtype)


VMEM = pl.BlockSpec(memory_space=pltpu.VMEM)
SMEM = pl.BlockSpec(memory_space=pltpu.SMEM)
HBM = pl.BlockSpec(memory_space=pltpu.HBM)
PARAMS = pltpu.CompilerParams(vmem_limit_bytes=20 * MIB)


def turned(value, axis, step):
    size = lax.axis_size(axis)
    return lax.ppermute(value, axis, [(i, (i + step) % size) for i in range(size)])


def on_device(images, valid_mask, row_kernel, col_kernel, exp_group, zero_point, psf_row, psf_col):
    _, visits, height, cols = images.shape
    inner = height - 2 * EDGE
    bands = lax.axis_size("band")
    strips = lax.axis_size("sky")
    above = turned(images[0, :, height - EDGE :, :], "sky", 1)
    below = turned(images[0, :, :EDGE, :], "sky", -1)

    lists = 2 * REJECT + 2
    inner_lists, part, edge_m, col_m, edge_mask = pl.pallas_call(
        inner_kernel,
        in_specs=[HBM] * 6,
        out_specs=[VMEM] * 5,
        out_shape=[
            vmem((lists, inner, cols)),
            vmem((visits, 2 * EDGE, cols)),
            vmem((visits, 4 * EDGE, LANES), BF16),
            vmem((visits, 2 * LANES, 2 * LANES), BF16),
            vmem((visits, 2 * EDGE, cols), jnp.int32),
        ],
        scratch_shapes=[
            pltpu.SMEM((1, visits), jnp.int32),
            pltpu.SMEM(zero_point.shape, F32),
            pltpu.VMEM((visits, 1, TAPS), F32),
            pltpu.VMEM((visits, 1, TAPS), F32),
            pltpu.VMEM((visits, height, cols), BF16),
            pltpu.VMEM((visits, height, cols), jnp.int32),
            pltpu.VMEM((16 * UNROLL, LANES), F32),
            pltpu.VMEM((visits, 2 * LANES, LANES), BF16),
            pltpu.VMEM((visits, inner, cols), F32),
            pltpu.SemaphoreType.DMA((4,)),
            pltpu.SemaphoreType.DMA((visits,)),
            pltpu.SemaphoreType.DMA((visits,)),
        ],
        compiler_params=PARAMS,
        cost_estimate=pl.CostEstimate(
            flops=visits * height * cols * 4096,
            bytes_accessed=visits * height * cols * 6,
            transcendentals=0,
        ),
        name="inner_visits",
    )(
        *(
            pltpu.with_memory_space_constraint(value, pltpu.HBM)
            for value in (
                exp_group,
                zero_point,
                images,
                valid_mask,
                row_kernel.transpose(1, 0, 2),
                col_kernel.transpose(1, 0, 2),
            )
        )
    )
    swap = [(0, 1), (1, 0)]
    held, _, _ = lax.optimization_barrier((inner_lists, above, below))
    inner_other = lax.ppermute(held, "exp", swap)

    edge_lists = pl.pallas_call(
        edge_kernel,
        in_specs=[VMEM] * 6,
        out_specs=VMEM,
        out_shape=vmem((lists, 2 * EDGE, cols)),
        scratch_shapes=[pltpu.VMEM((visits, 2 * EDGE, cols), F32)],
        compiler_params=PARAMS,
        name="edge_visits",
    )(above, below, part, edge_m, col_m, edge_mask)
    edge_other = lax.ppermute(edge_lists, "exp", swap)

    def merged(mine, other):
        rows = mine.shape[1]
        return pl.pallas_call(
            merge_kernel,
            in_specs=[VMEM, VMEM],
            out_specs=VMEM,
            out_shape=vmem((rows, cols)),
            compiler_params=PARAMS,
            name="merge",
        )(mine, other)

    edges = merged(edge_lists, edge_other)
    coadd_above = turned(edges[EDGE:].astype(BF16), "sky", 1)
    coadd_below = turned(edges[:EDGE].astype(BF16), "sky", -1)
    inner_coadd = merged(inner_lists, inner_other)

    width = cols // bands
    coadd_image, pieces = pl.pallas_call(
        psf_kernel,
        in_specs=[VMEM] * 6,
        out_specs=[VMEM, VMEM],
        out_shape=[vmem((1, height, cols)), vmem((bands, height + 8, width))],
        scratch_shapes=[pltpu.VMEM((16, LANES), F32)],
        compiler_params=PARAMS,
        name="psf",
    )(coadd_above, coadd_below, edges, inner_coadd, psf_row, psf_col)

    parts = [pieces[0]] + [turned(pieces[k], "band", k) for k in range(1, bands)]
    sums = jnp.stack([part[height:, :LANES] for part in parts])
    if strips <= 4:
        sums = sum((turned(sums, "sky", k) for k in range(1, strips)), sums)
    else:
        sums = lax.psum(sums, "sky")
    pixels = height * strips * cols
    detection = pl.pallas_call(
        lambda *refs: final_kernel(pixels, refs[:bands], refs[bands], refs[bands + 1]),
        in_specs=[VMEM] * (bands + 1),
        out_specs=VMEM,
        out_shape=vmem((height, width)),
        compiler_params=PARAMS,
        name="detection",
    )(*[part[:height] for part in parts], sums)
    return coadd_image, detection


def solution(mesh):
    placed = (
        P("band", "exp", ("patch", "sky"), None),
        P("band", "exp", ("patch", "sky"), None),
        P("band", "exp", None),
        P("band", "exp", None),
        P("band", "exp"),
        P("band", None),
        P("band", None),
        P("band", None),
    )
    return jax.shard_map(
        on_device,
        mesh=mesh,
        in_specs=placed,
        out_specs=(P("band", ("patch", "sky"), None), P(("patch", "sky"), "band")),
        check_vma=False,
    )
```

```python
import functools

import jax
import jax.numpy as jnp
from jax import lax
from jax.experimental import pallas as pl
from jax.experimental.pallas import tpu as pltpu
from jax.sharding import PartitionSpec as P

HALF = 15
REJECT = 4
TAPS = 31
EDGE = 16
LANES = 128
SENTINEL = 1e30
EPSILON = 1e-05
F32 = jnp.float32
BF16 = jnp.bfloat16
MIB = 1024 * 1024
UNROLL = 2


def split2(value):
    high = value.astype(BF16)
    return high, (value - high.astype(F32)).astype(BF16)


def band_rows(taps, rows):
    return pltpu.roll(
        jnp.broadcast_to(pltpu.roll(taps, 1, 1), (rows, LANES)), 0, 1, stride=1, stride_axis=0
    )


def around_matrix(taps):
    base = pltpu.roll(taps, LANES - HALF, 1)
    return pltpu.roll(jnp.broadcast_to(base, (LANES, LANES)), 0, 1, stride=1, stride_axis=0)


def square_masks():
    row = lax.broadcasted_iota(jnp.int32, (LANES, LANES), 0)
    col = lax.broadcasted_iota(jnp.int32, (LANES, LANES), 1)
    return row, col


def col_matrix(taps):
    return jnp.concatenate(split2(row_matrix(taps)), axis=0)


def row_matrix(taps):
    square = band_rows(taps, LANES)
    row, col = square_masks()
    return jnp.concatenate(
        [jnp.where(col > row, square, 0.0), jnp.where(col < row, square, 0.0)], axis=1
    )


def col_conv(value, matrix):
    rows, cols = value.shape
    tiles = cols // LANES
    turned = pltpu.roll(value, EDGE, 1)
    first = turned[:, :LANES]
    lane = lax.broadcasted_iota(jnp.int32, (rows, LANES), 1)
    wide = jnp.concatenate(
        [jnp.where(lane < EDGE, 0.0, first), turned[:, LANES:], jnp.where(lane < EDGE, first, 0.0)],
        axis=1,
    )
    parts = [
        part[:, n * LANES : (n + 2) * LANES] for part in split2(wide) for n in range(tiles)
    ]
    product = lax.dot_general(
        jnp.concatenate(parts, axis=0),
        matrix,
        (((1,), (1,)), ((), ())),
        preferred_element_type=F32,
    )

    def piece(n, side):
        return product[n * rows : (n + 1) * rows, side * LANES : (side + 1) * LANES]

    return jnp.concatenate(
        [piece(n, 0) + (piece(n, 1) + piece(tiles + n, 0)) for n in range(tiles)], axis=1
    )


def exchange(values, i, j):
    values[i], values[j] = (
        jnp.maximum(values[i], values[j]),
        jnp.minimum(values[i], values[j]),
    )


def cleaned(values):
    for i, j in ((0, 2), (1, 3), (0, 1), (2, 3)):
        exchange(values, i, j)
    return values


def top_sorted(values):
    best = None
    for start in range(0, len(values), REJECT):
        group = list(values[start : start + REJECT])
        if len(group) == 4:
            for i, j in ((0, 1), (2, 3), (0, 2), (1, 3), (1, 2)):
                exchange(group, i, j)
        elif len(group) == 3:
            for i, j in ((0, 1), (1, 2), (0, 1)):
                exchange(group, i, j)
        elif len(group) == 2:
            exchange(group, 0, 1)
        if best is None:
            best = group
        else:
            for i, value in enumerate(group):
                best[REJECT - 1 - i] = jnp.maximum(best[REJECT - 1 - i], value)
            best = cleaned(best)
    return best


def sort_visits(values, lists):
    visits, rows, cols = values.shape
    width = 2 * LANES

    def body(step, carry):
        at = pl.ds(pl.multiple_of(step * 8, 8), 8)
        for start in range(0, cols, width):
            lanes = pl.ds(start, width)
            low = [values[v, at, lanes] for v in range(visits)]
            dead = [value == SENTINEL for value in low]
            upper = top_sorted([jnp.where(d, -SENTINEL, v) for d, v in zip(dead, low)])
            total, count = 0.0, 0.0
            for d, v in zip(dead, low):
                total = total + jnp.where(d, 0.0, v)
                count = count + jnp.where(d, 0.0, 1.0)
            lower = top_sorted([-v for v in low])
            for i in range(REJECT):
                lists[i, at, lanes] = upper[i]
                lists[REJECT + i, at, lanes] = lower[i]
            lists[2 * REJECT, at, lanes] = total
            lists[2 * REJECT + 1, at, lanes] = count
        return carry

    lax.fori_loop(0, rows // 8, body, 0)


def at_ends(first, second):
    strip = lax.axis_index("sky")
    even = lax.rem(strip, 2) == 0
    top, bottom = strip == 0, strip == lax.axis_size("sky") - 1
    above, below = jnp.where(even, second, first), jnp.where(even, first, second)
    return (
        jnp.where(top, jnp.zeros_like(above), above),
        jnp.where(bottom, jnp.zeros_like(below), below),
    )


def inner_kernel(
    groups_h,
    points_h,
    images_h,
    mask_h,
    row_taps_h,
    col_taps_h,
    lists,
    part,
    edge_m,
    col_m,
    edge_mask,
    groups,
    points,
    row_taps,
    col_taps,
    images,
    mask,
    taps,
    row_m,
    values,
    small_sems,
    image_sems,
    mask_sems,
):
    visits, height, _ = images.shape
    small = [
        pltpu.make_async_copy(source, target, small_sems.at[i])
        for i, (source, target) in enumerate(
            ((groups_h, groups), (points_h, points), (row_taps_h, row_taps), (col_taps_h, col_taps))
        )
    ]

    middle = visits // 2 // UNROLL * UNROLL if visits % UNROLL == 0 else visits // 2

    def image_copy(i):
        at = pl.ds(0, middle) if i == 0 else pl.ds(middle, visits - middle)
        return pltpu.make_async_copy(images_h.at[0, at], images.at[at], image_sems.at[i])

    def mask_copy(i):
        at = pl.ds(0, middle) if i == 0 else pl.ds(middle, visits - middle)
        return pltpu.make_async_copy(mask_h.at[0, at], mask.at[at], mask_sems.at[i])

    for copy in small:
        copy.start()
    for i in range(2):
        image_copy(i).start()
        mask_copy(i).start()
    taps[...] = jnp.zeros_like(taps)
    row, col = square_masks()
    near = jnp.abs(row - col) <= HALF
    for copy in small:
        copy.wait()
    def build(v, slot):
        taps[slot : slot + 1, 0:TAPS] = row_taps[v]
        taps[slot + 8 : slot + 9, 0:TAPS] = col_taps[v]
        scale = points[0, groups[0, v]]
        square = around_matrix(taps[slot : slot + 1, :])
        row_m[v] = jnp.concatenate(split2(jnp.where(near, square, 0.0)), axis=1)
        far = jnp.where(near, 0.0, square)
        far = jnp.concatenate([far[:EDGE], far[height - EDGE :]], axis=0)
        edge_m[v] = jnp.concatenate(split2(far), axis=0)
        col_m[v] = col_matrix(taps[slot + 8 : slot + 9, :] * scale)

    def convolve(v, slot):
        image = images[v]
        smeared = jnp.dot(
            row_m[v], jnp.concatenate([image, image], axis=0), preferred_element_type=F32
        )
        part[v, 0:EDGE] = smeared[:EDGE]
        part[v, EDGE : 2 * EDGE] = smeared[height - EDGE :]
        result = col_conv(smeared[EDGE : height - EDGE], col_m[v])
        values[v] = jnp.where(mask[v, EDGE : height - EDGE] == 1, result, SENTINEL)
        edge_mask[v, 0:EDGE] = mask[v, 0:EDGE]
        edge_mask[v, EDGE : 2 * EDGE] = mask[v, height - EDGE :]

    at_once = UNROLL if visits % UNROLL == 0 else 1
    steps = visits // at_once

    def body(step, carry):
        for i in range(at_once):
            convolve(step * at_once + i, 16 * i)
        for i in range(at_once):
            build(lax.rem((step + 1) * at_once + i, visits), 16 * i)
        return carry

    for i in range(at_once):
        build(i, 16 * i)
    turn = middle // at_once
    for part_of, first, last in ((0, 0, turn), (1, turn, steps)):
        image_copy(part_of).wait()
        mask_copy(part_of).wait()
        lax.fori_loop(first, last, body, 0)
    sort_visits(values, lists)


def edge_kernel(first, second, part, edge_m, col_m, edge_mask, lists, values):
    visits, _, cols = values.shape
    for visit in range(visits):
        before, after = at_ends(first[visit], second[visit])
        window = jnp.concatenate(
            [after, jnp.zeros((LANES - 2 * EDGE, cols), BF16), before], axis=0
        )
        both = jnp.dot(edge_m[visit], window, preferred_element_type=F32)
        result = col_conv(part[visit] + (both[: 2 * EDGE] + both[2 * EDGE :]), col_m[visit])
        values[visit] = jnp.where(edge_mask[visit] == 1, result, SENTINEL)
    sort_visits(values, lists)


def merge_kernel(mine, other, coadd):
    def body(step, carry):
        at = pl.ds(pl.multiple_of(step * 8, 8), 8)
        upper, lower = 0.0, 0.0
        for i in range(REJECT):
            j = REJECT - 1 - i
            upper = upper + jnp.maximum(mine[i, at, :], other[j, at, :])
            lower = lower + jnp.maximum(mine[REJECT + i, at, :], other[REJECT + j, at, :])
        total = mine[2 * REJECT, at, :] + other[2 * REJECT, at, :]
        count = mine[2 * REJECT + 1, at, :] + other[2 * REJECT + 1, at, :]
        coadd[at, :] = (total - upper + lower) / (count - 2 * REJECT)
        return carry

    lax.fori_loop(0, coadd.shape[0] // 8, body, 0)


def edge_merge_kernel(mine, other, coadd, send_first, send_second):
    merge_kernel(mine, other, coadd)
    even = lax.rem(lax.axis_index("sky"), 2) == 0
    top, bottom = coadd[0:EDGE], coadd[EDGE : 2 * EDGE]
    send_first[...] = jnp.where(even, bottom, top).astype(BF16)
    send_second[...] = jnp.where(even, top, bottom).astype(BF16)


def psf_kernel(first, second, edges, inner, row_taps, col_taps, coadd, keep, send, taps, scratch):
    height, cols = coadd.shape[1:]
    width = keep.shape[1]
    others, half, _ = send.shape
    half = half - 8
    coadd[0, 0:EDGE] = edges[0:EDGE]
    coadd[0, EDGE : height - EDGE] = inner[...]
    coadd[0, height - EDGE : height] = edges[EDGE : 2 * EDGE]
    taps[...] = jnp.zeros_like(taps)
    taps[0:1, 0:TAPS] = row_taps[...]
    taps[8:9, 0:TAPS] = col_taps[...]
    row_h, row_l = split2(row_matrix(taps[0:1, :]))
    col_m = col_matrix(taps[8:9, :])
    mid_h, mid_l = split2(coadd[0])
    rest = jnp.zeros((2 * LANES - height - 2 * EDGE, cols), BF16)
    empty = jnp.zeros((EDGE, cols), BF16)
    before, after = at_ends(first[...], second[...])
    high = jnp.concatenate([before, mid_h, after, rest], axis=0)
    low = jnp.concatenate([empty, mid_l, empty, rest], axis=0)
    both = jnp.dot(jnp.concatenate([row_h, row_l], axis=0), high, preferred_element_type=F32)
    both_low = jnp.dot(row_h, low, preferred_element_type=F32)
    filtered = col_conv(both[:height] + (both[height:] + both_low), col_m)
    energy = filtered * filtered
    part = jnp.sum(energy.reshape(height // 8, 8, cols), axis=0)
    part = sum(part[:, n * LANES : (n + 1) * LANES] for n in range(cols // LANES))
    scratch[...] = energy
    own = lax.axis_index("band")
    start = pl.multiple_of(lax.axis_index("exp") * half, half)
    keep[0:height] = scratch[:, pl.ds(pl.multiple_of(own * width, width), width)]
    for k in range(others):
        band = lax.rem(own + k + 1, others + 1)
        lanes = pl.ds(pl.multiple_of(band * width, width), width)
        send[k, 0:half] = scratch[pl.ds(start, half), lanes]
    for n in range(width // LANES):
        keep[height : height + 8, n * LANES : (n + 1) * LANES] = part
        for k in range(others):
            send[k, half : half + 8, n * LANES : (n + 1) * LANES] = part


def final_kernel(pixels, keep, *refs):
    others = (len(refs) - 2) // 2
    mine, theirs, sums, detection = refs[:others], refs[others : 2 * others], refs[-2], refs[-1]
    height = detection.shape[0]
    half = height // 2
    scales = [1.0 / (jnp.sum(sums[i]) / pixels + EPSILON) for i in range(others + 1)]
    core = lax.axis_index("exp")
    for place, parts in ((core, mine), (1 - core, theirs)):
        at = pl.ds(pl.multiple_of(place * half, half), half)
        total = keep[at, :] * scales[0]
        for i in range(others):
            total = total + parts[i][0:half, :] * scales[i + 1]
        detection[at, :] = total


def vmem(shape, dtype=F32):
    return jax.ShapeDtypeStruct(shape, dtype)


VMEM = pl.BlockSpec(memory_space=pltpu.VMEM)
SMEM = pl.BlockSpec(memory_space=pltpu.SMEM)
HBM = pl.BlockSpec(memory_space=pltpu.HBM)
PARAMS = pltpu.CompilerParams(vmem_limit_bytes=20 * MIB)


def paired(value, start):
    strips, cores = lax.axis_size("sky"), lax.axis_size("exp")
    partner = {}
    for i in range(start, strips - 1, 2):
        partner[i], partner[i + 1] = i + 1, i
    pairs = []
    for strip in range(strips):
        for core in range(cores):
            to = (partner[strip], core) if strip in partner else (strip, cores - 1 - core)
            pairs.append((strip * cores + core, to[0] * cores + to[1]))
    return lax.ppermute(value, ("sky", "exp"), pairs)


def flipped(value, axis, bits):
    return lax.ppermute(value, axis, [(i, i ^ bits) for i in range(lax.axis_size(axis))])


def turned(value, axis, step):
    size = lax.axis_size(axis)
    return lax.ppermute(value, axis, [(i, (i + step) % size) for i in range(size)])


def on_device(images, valid_mask, row_kernel, col_kernel, exp_group, zero_point, psf_row, psf_col):
    _, visits, height, cols = images.shape
    inner = height - 2 * EDGE
    bands = lax.axis_size("band")
    strips = lax.axis_size("sky")
    even = lax.rem(lax.axis_index("sky"), 2) == 0
    far = jnp.where(even, height - EDGE, 0)
    first = paired(lax.dynamic_slice_in_dim(images[0], far, EDGE, 1), 0)
    second = paired(lax.dynamic_slice_in_dim(images[0], height - EDGE - far, EDGE, 1), 1)

    lists = 2 * REJECT + 2
    inner_lists, part, edge_m, col_m, edge_mask = pl.pallas_call(
        inner_kernel,
        in_specs=[HBM] * 6,
        out_specs=[VMEM] * 5,
        out_shape=[
            vmem((lists, inner, cols)),
            vmem((visits, 2 * EDGE, cols)),
            vmem((visits, 4 * EDGE, LANES), BF16),
            vmem((visits, 2 * LANES, 2 * LANES), BF16),
            vmem((visits, 2 * EDGE, cols), jnp.int32),
        ],
        scratch_shapes=[
            pltpu.SMEM((1, visits), jnp.int32),
            pltpu.SMEM(zero_point.shape, F32),
            pltpu.VMEM((visits, 1, TAPS), F32),
            pltpu.VMEM((visits, 1, TAPS), F32),
            pltpu.VMEM((visits, height, cols), BF16),
            pltpu.VMEM((visits, height, cols), jnp.int32),
            pltpu.VMEM((16 * UNROLL, LANES), F32),
            pltpu.VMEM((visits, LANES, 2 * LANES), BF16),
            pltpu.VMEM((visits, inner, cols), F32),
            pltpu.SemaphoreType.DMA((4,)),
            pltpu.SemaphoreType.DMA((2,)),
            pltpu.SemaphoreType.DMA((2,)),
        ],
        compiler_params=PARAMS,
        cost_estimate=pl.CostEstimate(
            flops=visits * height * cols * 4096,
            bytes_accessed=visits * height * cols * 6,
            transcendentals=0,
        ),
        name="inner_visits",
    )(
        *(
            pltpu.with_memory_space_constraint(value, pltpu.HBM)
            for value in (
                exp_group,
                zero_point,
                images,
                valid_mask,
                row_kernel.transpose(1, 0, 2),
                col_kernel.transpose(1, 0, 2),
            )
        )
    )
    swap = [(0, 1), (1, 0)]
    edge_lists = pl.pallas_call(
        edge_kernel,
        in_specs=[VMEM] * 6,
        out_specs=VMEM,
        out_shape=vmem((lists, 2 * EDGE, cols)),
        scratch_shapes=[pltpu.VMEM((visits, 2 * EDGE, cols), F32)],
        compiler_params=PARAMS,
        name="edge_visits",
    )(first, second, part, edge_m, col_m, edge_mask)
    edge_other = lax.ppermute(edge_lists, "exp", swap)

    held, _ = lax.optimization_barrier((inner_lists, edge_other))
    inner_other = lax.ppermute(held, "exp", swap)

    edges, send_first, send_second = pl.pallas_call(
        edge_merge_kernel,
        in_specs=[VMEM] * 2,
        out_specs=[VMEM] * 3,
        out_shape=[vmem((2 * EDGE, cols)), vmem((EDGE, cols), BF16), vmem((EDGE, cols), BF16)],
        compiler_params=PARAMS,
        name="edge_merge",
    )(edge_lists, edge_other)
    coadd_first = paired(send_first, 0)
    coadd_second = paired(send_second, 1)
    inner_coadd = pl.pallas_call(
        merge_kernel,
        in_specs=[VMEM] * 2,
        out_specs=VMEM,
        out_shape=vmem((inner, cols)),
        compiler_params=PARAMS,
        name="inner_merge",
    )(inner_lists, inner_other)

    width = cols // bands
    coadd_image, keep, send = pl.pallas_call(
        psf_kernel,
        in_specs=[VMEM] * 6,
        out_specs=[VMEM] * 3,
        out_shape=[
            vmem((1, height, cols)),
            vmem((height + 8, width)),
            vmem((bands - 1, height // 2 + 8, width)),
        ],
        scratch_shapes=[pltpu.VMEM((16, LANES), F32), pltpu.VMEM((height, cols), F32)],
        compiler_params=PARAMS,
        name="psf",
    )(coadd_first, coadd_second, edges, inner_coadd, psf_row, psf_col)

    if strips == 4 and bands == 2:
        power = keep[height:, :LANES]
        got = turned(send[0], "band", 1)
        mine, theirs = [got], [lax.ppermute(got, "exp", swap)]
        beside = flipped(power, "sky", 1)
        across = lax.ppermute(
            power, ("sky", "band"), [(2 * i + j, 2 * (i ^ 1) + 1 - j) for i in range(4) for j in (0, 1)]
        )
        sums = jnp.stack([power + beside, got[height // 2 :, :LANES] + across])
        sums = sums + flipped(sums, "sky", 2)
    else:
        mine = [turned(send[k - 1], "band", k) for k in range(1, bands)]
        theirs = [lax.ppermute(part, "exp", swap) for part in mine]
        sums = jnp.stack([keep[height:, :LANES]] + [part[height // 2 :, :LANES] for part in mine])
        sums = lax.psum(sums, "sky")
    pixels = height * strips * cols
    detection = pl.pallas_call(
        functools.partial(final_kernel, pixels),
        in_specs=[VMEM] * (2 * bands),
        out_specs=VMEM,
        out_shape=vmem((height, width)),
        compiler_params=PARAMS,
        name="detection",
    )(keep, *mine, *theirs, sums)
    return coadd_image, detection


def solution(mesh):
    placed = (
        P("band", "exp", ("patch", "sky"), None),
        P("band", "exp", ("patch", "sky"), None),
        P("band", "exp", None),
        P("band", "exp", None),
        P("band", "exp"),
        P("band", None),
        P("band", None),
        P("band", None),
    )
    return jax.shard_map(
        on_device,
        mesh=mesh,
        in_specs=placed,
        out_specs=(P("band", ("patch", "sky"), None), P(("patch", "sky"), "band")),
        check_vma=False,
    )
```

```python
import functools

import jax
import jax.numpy as jnp
from jax import lax
from jax.experimental import pallas as pl
from jax.experimental.pallas import tpu as pltpu
from jax.sharding import PartitionSpec as P

HALF = 15
REJECT = 4
TAPS = 31
EDGE = 16
LANES = 128
SENTINEL = 1e30
EPSILON = 1e-05
F32 = jnp.float32
BF16 = jnp.bfloat16
MIB = 1024 * 1024
UNROLL = 2


def split2(value):
    high = value.astype(BF16)
    return high, (value - high.astype(F32)).astype(BF16)


def band_rows(taps, rows):
    return pltpu.roll(
        jnp.broadcast_to(pltpu.roll(taps, 1, 1), (rows, LANES)), 0, 1, stride=1, stride_axis=0
    )


def around_matrix(taps):
    base = pltpu.roll(taps, LANES - HALF, 1)
    return pltpu.roll(jnp.broadcast_to(base, (LANES, LANES)), 0, 1, stride=1, stride_axis=0)


def square_masks():
    row = lax.broadcasted_iota(jnp.int32, (LANES, LANES), 0)
    col = lax.broadcasted_iota(jnp.int32, (LANES, LANES), 1)
    return row, col


def col_matrix(taps):
    return jnp.concatenate(split2(row_matrix(taps)), axis=0)


def row_matrix(taps):
    square = band_rows(taps, LANES)
    row, col = square_masks()
    return jnp.concatenate(
        [jnp.where(col > row, square, 0.0), jnp.where(col < row, square, 0.0)], axis=1
    )


def col_conv(value, matrix):
    rows, cols = value.shape
    tiles = cols // LANES
    turned = pltpu.roll(value, EDGE, 1)
    first = turned[:, :LANES]
    lane = lax.broadcasted_iota(jnp.int32, (rows, LANES), 1)
    wide = jnp.concatenate(
        [jnp.where(lane < EDGE, 0.0, first), turned[:, LANES:], jnp.where(lane < EDGE, first, 0.0)],
        axis=1,
    )
    parts = [
        part[:, n * LANES : (n + 2) * LANES] for part in split2(wide) for n in range(tiles)
    ]
    product = lax.dot_general(
        jnp.concatenate(parts, axis=0),
        matrix,
        (((1,), (1,)), ((), ())),
        preferred_element_type=F32,
    )

    def piece(n, side):
        return product[n * rows : (n + 1) * rows, side * LANES : (side + 1) * LANES]

    return jnp.concatenate(
        [piece(n, 0) + (piece(n, 1) + piece(tiles + n, 0)) for n in range(tiles)], axis=1
    )


def exchange(values, i, j):
    values[i], values[j] = (
        jnp.maximum(values[i], values[j]),
        jnp.minimum(values[i], values[j]),
    )


def cleaned(values):
    for i, j in ((0, 2), (1, 3), (0, 1), (2, 3)):
        exchange(values, i, j)
    return values


def top_sorted(values):
    best = None
    for start in range(0, len(values), REJECT):
        group = list(values[start : start + REJECT])
        if len(group) == 4:
            for i, j in ((0, 1), (2, 3), (0, 2), (1, 3), (1, 2)):
                exchange(group, i, j)
        elif len(group) == 3:
            for i, j in ((0, 1), (1, 2), (0, 1)):
                exchange(group, i, j)
        elif len(group) == 2:
            exchange(group, 0, 1)
        if best is None:
            best = group
        else:
            for i, value in enumerate(group):
                best[REJECT - 1 - i] = jnp.maximum(best[REJECT - 1 - i], value)
            best = cleaned(best)
    return best


def sort_visits(values, lists):
    visits, rows, cols = values.shape
    width = 2 * LANES

    def body(step, carry):
        at = pl.ds(pl.multiple_of(step * 8, 8), 8)
        for start in range(0, cols, width):
            lanes = pl.ds(start, width)
            low = [values[v, at, lanes] for v in range(visits)]
            dead = [value == SENTINEL for value in low]
            upper = top_sorted([jnp.where(d, -SENTINEL, v) for d, v in zip(dead, low)])
            total, count = 0.0, 0.0
            for d, v in zip(dead, low):
                total = total + jnp.where(d, 0.0, v)
                count = count + jnp.where(d, 0.0, 1.0)
            lower = top_sorted([-v for v in low])
            for i in range(REJECT):
                lists[i, at, lanes] = upper[i]
                lists[REJECT + i, at, lanes] = lower[i]
            lists[2 * REJECT, at, lanes] = total
            lists[2 * REJECT + 1, at, lanes] = count
        return carry

    lax.fori_loop(0, rows // 8, body, 0)


def at_ends(first, second):
    strip = lax.axis_index("sky")
    even = lax.rem(strip, 2) == 0
    top, bottom = strip == 0, strip == lax.axis_size("sky") - 1
    above, below = jnp.where(even, second, first), jnp.where(even, first, second)
    return (
        jnp.where(top, jnp.zeros_like(above), above),
        jnp.where(bottom, jnp.zeros_like(below), below),
    )


def inner_kernel(
    groups_h,
    points_h,
    images_h,
    mask_h,
    row_taps_h,
    col_taps_h,
    lists,
    part,
    edge_m,
    col_m,
    edge_mask,
    groups,
    points,
    row_taps,
    col_taps,
    images,
    mask,
    taps,
    row_m,
    values,
    small_sems,
    image_sems,
    mask_sems,
):
    visits, height, _ = images.shape
    small = [
        pltpu.make_async_copy(source, target, small_sems.at[i])
        for i, (source, target) in enumerate(
            ((groups_h, groups), (points_h, points), (row_taps_h, row_taps), (col_taps_h, col_taps))
        )
    ]

    middle = visits // 2 // UNROLL * UNROLL if visits % UNROLL == 0 else visits // 2

    def image_copy(i):
        at = pl.ds(0, middle) if i == 0 else pl.ds(middle, visits - middle)
        return pltpu.make_async_copy(images_h.at[0, at], images.at[at], image_sems.at[i])

    def mask_copy(i):
        at = pl.ds(0, middle) if i == 0 else pl.ds(middle, visits - middle)
        return pltpu.make_async_copy(mask_h.at[0, at], mask.at[at], mask_sems.at[i])

    for copy in small:
        copy.start()
    for i in range(2):
        image_copy(i).start()
        mask_copy(i).start()
    taps[...] = jnp.zeros_like(taps)
    row, col = square_masks()
    near = jnp.abs(row - col) <= HALF
    for copy in small:
        copy.wait()
    def build(v, slot):
        taps[slot : slot + 1, 0:TAPS] = row_taps[v]
        taps[slot + 8 : slot + 9, 0:TAPS] = col_taps[v]
        scale = points[0, groups[0, v]]
        square = around_matrix(taps[slot : slot + 1, :])
        row_m[v] = jnp.concatenate(split2(jnp.where(near, square, 0.0)), axis=1)
        far = jnp.where(near, 0.0, square)
        far = pltpu.roll(jnp.concatenate([far[:EDGE], far[height - EDGE :]], axis=0), EDGE, 1)
        edge_m[v] = jnp.concatenate(split2(far), axis=0)
        col_m[v] = col_matrix(taps[slot + 8 : slot + 9, :] * scale)

    def smear(v):
        image = images[v]
        smeared = jnp.dot(
            row_m[v], jnp.concatenate([image, image], axis=0), preferred_element_type=F32
        )
        values[v] = smeared[EDGE : height - EDGE]
        part[v, 0:EDGE] = smeared[:EDGE]
        part[v, EDGE : 2 * EDGE] = smeared[height - EDGE :]

    def convolve(v):
        result = col_conv(values[v], col_m[v])
        values[v] = jnp.where(mask[v, EDGE : height - EDGE] == 1, result, SENTINEL)
        edge_mask[v, 0:EDGE] = mask[v, 0:EDGE]
        edge_mask[v, EDGE : 2 * EDGE] = mask[v, height - EDGE :]

    at_once = UNROLL if visits % UNROLL == 0 else 1
    steps = visits // at_once

    def work(step, most=None):
        for i in range(at_once):
            convolve(step * at_once + i)
        for i in range(at_once):
            if most is None or most >= 1:
                smear((step + 1) * at_once + i)
        for i in range(at_once):
            if most is None or most >= 2:
                build((step + 2) * at_once + i, 16 * i)

    for step in range(min(2, steps)):
        for i in range(at_once):
            build(step * at_once + i, 16 * i)
    image_copy(0).wait()
    mask_copy(0).wait()
    for i in range(at_once):
        smear(i)
    early = max(min(middle // at_once - 1, steps - 2), 0)

    def body(step, carry):
        work(step)
        return carry

    lax.fori_loop(0, early, body, 0)
    image_copy(1).wait()
    mask_copy(1).wait()
    lax.fori_loop(early, steps - 2, body, 0)
    for step in range(max(steps - 2, 0), steps):
        work(step, steps - 1 - step)
    sort_visits(values, lists)


def edge_kernel(first, second, part, edge_m, col_m, edge_mask, lists, values):
    visits, _, cols = values.shape
    for visit in range(visits):
        before, after = at_ends(first[visit], second[visit])
        window = jnp.concatenate([before, after], axis=0)
        both = jnp.dot(edge_m[visit, :, 0 : 2 * EDGE], window, preferred_element_type=F32)
        values[visit] = part[visit] + (both[: 2 * EDGE] + both[2 * EDGE :])
    for visit in range(visits):
        result = col_conv(values[visit], col_m[visit])
        values[visit] = jnp.where(edge_mask[visit] == 1, result, SENTINEL)
    sort_visits(values, lists)


def merge_kernel(mine, other, coadd):
    def body(step, carry):
        at = pl.ds(pl.multiple_of(step * 8, 8), 8)
        upper, lower = 0.0, 0.0
        for i in range(REJECT):
            j = REJECT - 1 - i
            upper = upper + jnp.maximum(mine[i, at, :], other[j, at, :])
            lower = lower + jnp.maximum(mine[REJECT + i, at, :], other[REJECT + j, at, :])
        total = mine[2 * REJECT, at, :] + other[2 * REJECT, at, :]
        count = mine[2 * REJECT + 1, at, :] + other[2 * REJECT + 1, at, :]
        coadd[at, :] = (total - upper + lower) / (count - 2 * REJECT)
        return carry

    lax.fori_loop(0, coadd.shape[0] // 8, body, 0)


def edge_merge_kernel(mine, other, coadd, send_first, send_second):
    merge_kernel(mine, other, coadd)
    even = lax.rem(lax.axis_index("sky"), 2) == 0
    top, bottom = coadd[0:EDGE], coadd[EDGE : 2 * EDGE]
    send_first[...] = jnp.where(even, bottom, top).astype(BF16)
    send_second[...] = jnp.where(even, top, bottom).astype(BF16)


def psf_kernel(first, second, edges, inner, row_taps, col_taps, coadd, energy, power, taps):
    height, cols = coadd.shape[1:]
    coadd[0, 0:EDGE] = edges[0:EDGE]
    coadd[0, EDGE : height - EDGE] = inner[...]
    coadd[0, height - EDGE : height] = edges[EDGE : 2 * EDGE]
    taps[...] = jnp.zeros_like(taps)
    taps[0:1, 0:TAPS] = row_taps[...]
    taps[8:9, 0:TAPS] = col_taps[...]
    row_h, row_l = split2(row_matrix(taps[0:1, :]))
    col_m = col_matrix(taps[8:9, :])
    mid_h, mid_l = split2(coadd[0])
    rest = jnp.zeros((2 * LANES - height - 2 * EDGE, cols), BF16)
    empty = jnp.zeros((EDGE, cols), BF16)
    before, after = at_ends(first[...], second[...])
    high = jnp.concatenate([before, mid_h, after, rest], axis=0)
    low = jnp.concatenate([empty, mid_l, empty, rest], axis=0)
    both = jnp.dot(jnp.concatenate([row_h, row_l], axis=0), high, preferred_element_type=F32)
    both_low = jnp.dot(row_h, low, preferred_element_type=F32)
    filtered = col_conv(both[:height] + (both[height:] + both_low), col_m)
    squares = filtered * filtered
    energy[...] = squares
    part = jnp.sum(squares.reshape(height // 8, 8, cols), axis=0)
    power[...] = sum(part[:, n * LANES : (n + 1) * LANES] for n in range(cols // LANES))


def pack_kernel(energy, power, send):
    others, half, width = send.shape
    half = half - 8
    own = lax.axis_index("band")
    start = pl.multiple_of(lax.axis_index("exp") * half, half)
    for k in range(others):
        band = lax.rem(own + k + 1, others + 1)
        lanes = pl.ds(pl.multiple_of(band * width, width), width)
        send[k, 0:half] = energy[pl.ds(start, half), lanes]
        for n in range(width // LANES):
            send[k, half : half + 8, n * LANES : (n + 1) * LANES] = power[...]


def final_kernel(pixels, energy, *refs):
    others = (len(refs) - 2) // 2
    mine, theirs, sums, detection = refs[:others], refs[others : 2 * others], refs[-2], refs[-1]
    height, width = detection.shape
    half = height // 2
    lanes = pl.ds(pl.multiple_of(lax.axis_index("band") * width, width), width)
    scales = [1.0 / (jnp.sum(sums[i]) / pixels + EPSILON) for i in range(others + 1)]
    core = lax.axis_index("exp")
    for place, parts in ((core, mine), (1 - core, theirs)):
        at = pl.ds(pl.multiple_of(place * half, half), half)
        total = energy[at, lanes] * scales[0]
        for i in range(others):
            total = total + parts[i][0:half, :] * scales[i + 1]
        detection[at, :] = total


def vmem(shape, dtype=F32):
    return jax.ShapeDtypeStruct(shape, dtype)


VMEM = pl.BlockSpec(memory_space=pltpu.VMEM)
SMEM = pl.BlockSpec(memory_space=pltpu.SMEM)
HBM = pl.BlockSpec(memory_space=pltpu.HBM)
PARAMS = pltpu.CompilerParams(vmem_limit_bytes=20 * MIB)


def paired(value, start):
    strips, cores = lax.axis_size("sky"), lax.axis_size("exp")
    partner = {}
    for i in range(start, strips - 1, 2):
        partner[i], partner[i + 1] = i + 1, i
    pairs = []
    for strip in range(strips):
        for core in range(cores):
            to = (partner[strip], core) if strip in partner else (strip, cores - 1 - core)
            pairs.append((strip * cores + core, to[0] * cores + to[1]))
    return lax.ppermute(value, ("sky", "exp"), pairs)


def flipped(value, axis, bits):
    return lax.ppermute(value, axis, [(i, i ^ bits) for i in range(lax.axis_size(axis))])


def turned(value, axis, step):
    size = lax.axis_size(axis)
    return lax.ppermute(value, axis, [(i, (i + step) % size) for i in range(size)])


def on_device(images, valid_mask, row_kernel, col_kernel, exp_group, zero_point, psf_row, psf_col):
    _, visits, height, cols = images.shape
    inner = height - 2 * EDGE
    bands = lax.axis_size("band")
    strips = lax.axis_size("sky")
    even = lax.rem(lax.axis_index("sky"), 2) == 0
    far = jnp.where(even, height - EDGE, 0)
    first = paired(lax.dynamic_slice_in_dim(images[0], far, EDGE, 1), 0)
    second = paired(lax.dynamic_slice_in_dim(images[0], height - EDGE - far, EDGE, 1), 1)

    lists = 2 * REJECT + 2
    inner_lists, part, edge_m, col_m, edge_mask = pl.pallas_call(
        inner_kernel,
        in_specs=[HBM] * 6,
        out_specs=[VMEM] * 5,
        out_shape=[
            vmem((lists, inner, cols)),
            vmem((visits, 2 * EDGE, cols)),
            vmem((visits, 4 * EDGE, LANES), BF16),
            vmem((visits, 2 * LANES, 2 * LANES), BF16),
            vmem((visits, 2 * EDGE, cols), jnp.int32),
        ],
        scratch_shapes=[
            pltpu.SMEM((1, visits), jnp.int32),
            pltpu.SMEM(zero_point.shape, F32),
            pltpu.VMEM((visits, 1, TAPS), F32),
            pltpu.VMEM((visits, 1, TAPS), F32),
            pltpu.VMEM((visits, height, cols), BF16),
            pltpu.VMEM((visits, height, cols), jnp.int32),
            pltpu.VMEM((16 * UNROLL, LANES), F32),
            pltpu.VMEM((visits, LANES, 2 * LANES), BF16),
            pltpu.VMEM((visits, inner, cols), F32),
            pltpu.SemaphoreType.DMA((4,)),
            pltpu.SemaphoreType.DMA((2,)),
            pltpu.SemaphoreType.DMA((2,)),
        ],
        compiler_params=PARAMS,
        cost_estimate=pl.CostEstimate(
            flops=visits * height * cols * 4096,
            bytes_accessed=visits * height * cols * 6,
            transcendentals=0,
        ),
        name="inner_visits",
    )(
        *(
            pltpu.with_memory_space_constraint(value, pltpu.HBM)
            for value in (
                exp_group,
                zero_point,
                images,
                valid_mask,
                row_kernel.transpose(1, 0, 2),
                col_kernel.transpose(1, 0, 2),
            )
        )
    )
    swap = [(0, 1), (1, 0)]
    edge_lists = pl.pallas_call(
        edge_kernel,
        in_specs=[VMEM] * 6,
        out_specs=VMEM,
        out_shape=vmem((lists, 2 * EDGE, cols)),
        scratch_shapes=[pltpu.VMEM((visits, 2 * EDGE, cols), F32)],
        compiler_params=PARAMS,
        name="edge_visits",
    )(first, second, part, edge_m, col_m, edge_mask)
    edge_other = lax.ppermute(edge_lists, "exp", swap)

    held, _ = lax.optimization_barrier((inner_lists, edge_other))
    inner_other = lax.ppermute(held, "exp", swap)

    edges, send_first, send_second = pl.pallas_call(
        edge_merge_kernel,
        in_specs=[VMEM] * 2,
        out_specs=[VMEM] * 3,
        out_shape=[vmem((2 * EDGE, cols)), vmem((EDGE, cols), BF16), vmem((EDGE, cols), BF16)],
        compiler_params=PARAMS,
        name="edge_merge",
    )(edge_lists, edge_other)
    coadd_first = paired(send_first, 0)
    coadd_second = paired(send_second, 1)
    inner_coadd = pl.pallas_call(
        merge_kernel,
        in_specs=[VMEM] * 2,
        out_specs=VMEM,
        out_shape=vmem((inner, cols)),
        compiler_params=PARAMS,
        name="inner_merge",
    )(inner_lists, inner_other)

    width = cols // bands
    coadd_image, energy, power = pl.pallas_call(
        psf_kernel,
        in_specs=[VMEM] * 6,
        out_specs=[VMEM] * 3,
        out_shape=[
            vmem((1, height, cols)),
            vmem((height, cols)),
            vmem((8, LANES)),
        ],
        scratch_shapes=[pltpu.VMEM((16, LANES), F32)],
        compiler_params=PARAMS,
        name="psf",
    )(coadd_first, coadd_second, edges, inner_coadd, psf_row, psf_col)
    send = pl.pallas_call(
        pack_kernel,
        in_specs=[VMEM] * 2,
        out_specs=VMEM,
        out_shape=vmem((bands - 1, height // 2 + 8, width)),
        compiler_params=PARAMS,
        name="pack",
    )(energy, power)

    if strips == 4 and bands == 2 and lax.axis_size("exp") == 2:
        pairs = []
        for strip in range(strips):
            for core in range(2):
                for band in range(2):
                    to = (strip ^ 1, core, band ^ core)
                    pairs.append((4 * strip + 2 * core + band, 4 * to[0] + 2 * to[1] + to[2]))
        one = lax.ppermute(power, ("sky", "exp", "band"), pairs)
        two = lax.ppermute(one, "exp", swap)
        first_core = lax.axis_index("exp") == 0
        beside, across = jnp.where(first_core, one, two), jnp.where(first_core, two, one)
        got = turned(send[0], "band", 1)
        mine, theirs = [got], [lax.ppermute(got, "exp", swap)]
        sums = jnp.stack([power + beside, got[height // 2 :, :LANES] + across])
        sums = sums + flipped(sums, "sky", 2)
    else:
        mine = [turned(send[k - 1], "band", k) for k in range(1, bands)]
        theirs = [lax.ppermute(part, "exp", swap) for part in mine]
        sums = jnp.stack([power] + [part[height // 2 :, :LANES] for part in mine])
        sums = lax.psum(sums, "sky")
    pixels = height * strips * cols
    detection = pl.pallas_call(
        functools.partial(final_kernel, pixels),
        in_specs=[VMEM] * (2 * bands),
        out_specs=VMEM,
        out_shape=vmem((height, width)),
        compiler_params=PARAMS,
        name="detection",
    )(energy, *mine, *theirs, sums)
    return coadd_image, detection


def solution(mesh):
    placed = (
        P("band", "exp", ("patch", "sky"), None),
        P("band", "exp", ("patch", "sky"), None),
        P("band", "exp", None),
        P("band", "exp", None),
        P("band", "exp"),
        P("band", None),
        P("band", None),
        P("band", None),
    )
    return jax.shard_map(
        on_device,
        mesh=mesh,
        in_specs=placed,
        out_specs=(P("band", ("patch", "sky"), None), P(("patch", "sky"), "band")),
        check_vma=False,
    )
```

```python
import functools

import jax
import jax.numpy as jnp
from jax import lax
from jax.experimental import pallas as pl
from jax.experimental.pallas import tpu as pltpu
from jax.sharding import PartitionSpec as P

HALF = 15
REJECT = 4
TAPS = 31
EDGE = 16
LANES = 128
SENTINEL = 1e30
EPSILON = 1e-05
F32 = jnp.float32
BF16 = jnp.bfloat16
MIB = 1024 * 1024
UNROLL = 2


def split2(value):
    high = value.astype(BF16)
    return high, (value - high.astype(F32)).astype(BF16)


def band_rows(taps, rows):
    return pltpu.roll(
        jnp.broadcast_to(pltpu.roll(taps, 1, 1), (rows, LANES)), 0, 1, stride=1, stride_axis=0
    )


def around_matrix(taps):
    base = pltpu.roll(taps, LANES - HALF, 1)
    return pltpu.roll(jnp.broadcast_to(base, (LANES, LANES)), 0, 1, stride=1, stride_axis=0)


def square_masks():
    row = lax.broadcasted_iota(jnp.int32, (LANES, LANES), 0)
    col = lax.broadcasted_iota(jnp.int32, (LANES, LANES), 1)
    return row, col


def col_matrix(taps):
    return jnp.concatenate(split2(row_matrix(taps)), axis=0)


def row_matrix(taps):
    square = band_rows(taps, LANES)
    row, col = square_masks()
    return jnp.concatenate(
        [jnp.where(col > row, square, 0.0), jnp.where(col < row, square, 0.0)], axis=1
    )


def col_conv(value, matrix):
    rows, cols = value.shape
    tiles = cols // LANES
    turned = pltpu.roll(value, EDGE, 1)
    first = turned[:, :LANES]
    lane = lax.broadcasted_iota(jnp.int32, (rows, LANES), 1)
    wide = jnp.concatenate(
        [jnp.where(lane < EDGE, 0.0, first), turned[:, LANES:], jnp.where(lane < EDGE, first, 0.0)],
        axis=1,
    )
    parts = [
        part[:, n * LANES : (n + 2) * LANES] for part in split2(wide) for n in range(tiles)
    ]
    product = lax.dot_general(
        jnp.concatenate(parts, axis=0),
        matrix,
        (((1,), (1,)), ((), ())),
        preferred_element_type=F32,
    )

    def piece(n, side):
        return product[n * rows : (n + 1) * rows, side * LANES : (side + 1) * LANES]

    return jnp.concatenate(
        [piece(n, 0) + (piece(n, 1) + piece(tiles + n, 0)) for n in range(tiles)], axis=1
    )


def ordered(values, pairs, first, second):
    values = list(values)
    for i, j in pairs:
        values[i], values[j] = first(values[i], values[j]), second(values[i], values[j])
    return values


def foremost(groups, first, second):
    best = None
    while groups:
        group, groups = groups[0], groups[1:]
        if len(group) == 2 and groups and len(groups[0]) == 2:
            group, groups = [*group, *groups[0]], groups[1:]
            group = ordered(group, ((0, 2), (1, 3), (1, 2)), first, second)
        if best is None:
            best = group
        elif len(best) < REJECT:
            best = best + group
            pairs = [(j, j + 1) for i in range(len(best)) for j in range(len(best) - 1 - i)]
            best = ordered(best, pairs, first, second)[:REJECT]
        else:
            best = list(best)
            for i, value in enumerate(group):
                best[REJECT - 1 - i] = first(best[REJECT - 1 - i], value)
            best = ordered(best, ((0, 2), (1, 3), (0, 1), (2, 3)), first, second)
    return best


def hold(visit, results, masks, upper, lower, totals, counts):
    masks = [mask for mask in masks]
    usable = [mask == 1 for mask in masks]
    tops = [jnp.where(use, value, -SENTINEL) for use, value in zip(usable, results)]
    ends = [jnp.where(use, value, SENTINEL) for use, value in zip(usable, results)]
    if len(results) == 2:
        tops = ordered(tops, ((0, 1),), jnp.maximum, jnp.minimum)
        ends = ordered(ends, ((0, 1),), jnp.minimum, jnp.maximum)
    for i in range(len(results)):
        upper[visit + i] = tops[i]
        lower[visit + i] = ends[i]
    totals[...] += sum(jnp.where(use, value, 0.0) for use, value in zip(usable, results))
    counts[...] += sum(masks)


def sort_visits(at_once, upper, lower, totals, counts, start, lists):
    visits, _, cols = upper.shape
    rows = lists.shape[1]
    width = 2 * LANES

    def body(step, carry):
        at = pl.ds(pl.multiple_of(step * 8, 8), 8)
        source = pl.ds(pl.multiple_of(step * 8 + start, 8), 8)
        for left in range(0, cols, width):
            lanes = pl.ds(left, width)
            for place, values, first, second in (
                (0, upper, jnp.maximum, jnp.minimum),
                (REJECT, lower, jnp.minimum, jnp.maximum),
            ):
                groups = [
                    [values[v + i, source, lanes] for i in range(at_once)]
                    for v in range(0, visits, at_once)
                ]
                for i, value in enumerate(foremost(groups, first, second)):
                    lists[place + i, at, lanes] = value
            lists[2 * REJECT, at, lanes] = totals[source, lanes]
            lists[2 * REJECT + 1, at, lanes] = counts[source, lanes].astype(F32)
        return carry

    lax.fori_loop(0, rows // 8, body, 0)


def inner_kernel(
    groups_h,
    points_h,
    images_h,
    mask_h,
    row_taps_h,
    col_taps_h,
    early_lists,
    late_lists,
    part,
    edge_m,
    col_m,
    edge_mask,
    groups,
    points,
    row_taps,
    col_taps,
    images,
    mask,
    taps,
    row_m,
    values,
    upper,
    lower,
    totals,
    counts,
    small_sems,
    image_sems,
    mask_sems,
):
    visits, height, _ = images.shape
    small = [
        pltpu.make_async_copy(source, target, small_sems.at[i])
        for i, (source, target) in enumerate(
            ((groups_h, groups), (points_h, points), (row_taps_h, row_taps), (col_taps_h, col_taps))
        )
    ]

    middle = visits // 2 // UNROLL * UNROLL if visits % UNROLL == 0 else visits // 2

    def image_copy(i):
        at = pl.ds(0, middle) if i == 0 else pl.ds(middle, visits - middle)
        return pltpu.make_async_copy(images_h.at[0, at], images.at[at], image_sems.at[i])

    def mask_copy(i):
        at = pl.ds(0, middle) if i == 0 else pl.ds(middle, visits - middle)
        return pltpu.make_async_copy(mask_h.at[0, at], mask.at[at], mask_sems.at[i])

    for copy in small:
        copy.start()
    for i in range(2):
        image_copy(i).start()
        mask_copy(i).start()
    taps[...] = jnp.zeros_like(taps)
    totals[...] = jnp.zeros_like(totals)
    counts[...] = jnp.zeros_like(counts)
    row, col = square_masks()
    near = jnp.abs(row - col) <= HALF
    for copy in small:
        copy.wait()
    def build(v, slot):
        taps[slot : slot + 1, 0:TAPS] = row_taps[v]
        taps[slot + 8 : slot + 9, 0:TAPS] = col_taps[v]
        scale = points[0, groups[0, v]]
        square = around_matrix(taps[slot : slot + 1, :])
        row_m[v] = jnp.concatenate(split2(jnp.where(near, square, 0.0)), axis=1)
        far = jnp.where(near, 0.0, square)
        far = pltpu.roll(jnp.concatenate([far[:EDGE], far[height - EDGE :]], axis=0), EDGE, 1)
        edge_m[v] = jnp.concatenate(split2(far), axis=0)
        col_m[v] = col_matrix(taps[slot + 8 : slot + 9, :] * scale)

    def smear(v):
        image = images[v]
        smeared = jnp.dot(
            row_m[v], jnp.concatenate([image, image], axis=0), preferred_element_type=F32
        )
        values[v] = smeared[EDGE : height - EDGE]
        part[v, 0:EDGE] = smeared[:EDGE]
        part[v, EDGE : 2 * EDGE] = smeared[height - EDGE :]

    def convolve(v, number):
        results = [col_conv(values[v + i], col_m[v + i]) for i in range(number)]
        masks = [mask[v + i, EDGE : height - EDGE] for i in range(number)]
        hold(v, results, masks, upper, lower, totals, counts)
        for i in range(number):
            edge_mask[v + i, 0:EDGE] = mask[v + i, 0:EDGE]
            edge_mask[v + i, EDGE : 2 * EDGE] = mask[v + i, height - EDGE :]

    at_once = UNROLL if visits % UNROLL == 0 else 1
    steps = visits // at_once

    def work(step, most=None):
        convolve(step * at_once, at_once)
        for i in range(at_once):
            if most is None or most >= 1:
                smear((step + 1) * at_once + i)
        for i in range(at_once):
            if most is None or most >= 2:
                build((step + 2) * at_once + i, 16 * i)

    for step in range(min(2, steps)):
        for i in range(at_once):
            build(step * at_once + i, 16 * i)
    image_copy(0).wait()
    mask_copy(0).wait()
    for i in range(at_once):
        smear(i)
    ready = max(min(middle // at_once - 1, steps - 2), 0)

    def body(step, carry):
        work(step)
        return carry

    lax.fori_loop(0, ready, body, 0)
    image_copy(1).wait()
    mask_copy(1).wait()
    lax.fori_loop(ready, steps - 2, body, 0)
    for step in range(max(steps - 2, 0), steps):
        work(step, steps - 1 - step)
    held = (at_once, upper, lower, totals, counts)
    sort_visits(*held, 0, early_lists)
    sort_visits(*held, early_lists.shape[1], late_lists)


def at_ends(first, second):
    strip = lax.axis_index("sky")
    even = lax.rem(strip, 2) == 0
    top, bottom = strip == 0, strip == lax.axis_size("sky") - 1
    above, below = jnp.where(even, second, first), jnp.where(even, first, second)
    return (
        jnp.where(top, jnp.zeros_like(above), above),
        jnp.where(bottom, jnp.zeros_like(below), below),
    )


def edge_kernel(
    first, second, part, edge_m, col_m, edge_mask, lists, values, upper, lower, totals, counts
):
    visits, _, cols = values.shape
    for visit in range(visits):
        before, after = at_ends(first[visit], second[visit])
        window = jnp.concatenate([before, after], axis=0)
        both = jnp.dot(edge_m[visit, :, 0 : 2 * EDGE], window, preferred_element_type=F32)
        values[visit] = part[visit] + (both[: 2 * EDGE] + both[2 * EDGE :])
    at_once = UNROLL if visits % UNROLL == 0 else 1
    totals[...] = jnp.zeros_like(totals)
    counts[...] = jnp.zeros_like(counts)
    for visit in range(0, visits, at_once):
        results = [col_conv(values[visit + i], col_m[visit + i]) for i in range(at_once)]
        masks = [edge_mask[visit + i] for i in range(at_once)]
        hold(visit, results, masks, upper, lower, totals, counts)
    sort_visits(at_once, upper, lower, totals, counts, 0, lists)


def merge(mine, other, coadd, start):
    def body(step, carry):
        at = pl.ds(pl.multiple_of(step * 8, 8), 8)
        upper, lower = 0.0, 0.0
        for i in range(REJECT):
            j = REJECT - 1 - i
            upper = upper + jnp.maximum(mine[i, at, :], other[j, at, :])
            lower = lower + jnp.minimum(mine[REJECT + i, at, :], other[REJECT + j, at, :])
        total = mine[2 * REJECT, at, :] + other[2 * REJECT, at, :]
        count = mine[2 * REJECT + 1, at, :] + other[2 * REJECT + 1, at, :]
        coadd[pl.ds(pl.multiple_of(step * 8 + start, 8), 8), :] = (total - upper - lower) / (
            count - 2 * REJECT
        )
        return carry

    lax.fori_loop(0, mine.shape[1] // 8, body, 0)


def edge_merge_kernel(mine, other, coadd, send_first, send_second):
    merge(mine, other, coadd, 0)
    even = lax.rem(lax.axis_index("sky"), 2) == 0
    top, bottom = coadd[0:EDGE], coadd[EDGE : 2 * EDGE]
    send_first[...] = jnp.where(even, bottom, top).astype(BF16)
    send_second[...] = jnp.where(even, top, bottom).astype(BF16)


def lane_sums(squares):
    rows, cols = squares.shape
    part = jnp.sum(squares.reshape(rows // 8, 8, cols), axis=0)
    return sum(part[:, n * LANES : (n + 1) * LANES] for n in range(cols // LANES))


def inner_psf_kernel(
    early_mine,
    early_other,
    late_mine,
    late_other,
    edges,
    row_taps,
    col_taps,
    coadd,
    energy,
    power,
    part,
    edge_m,
    col_m,
    taps,
):
    height = coadd.shape[1]
    merge(early_mine, early_other, coadd.at[0], EDGE)
    merge(late_mine, late_other, coadd.at[0], EDGE + early_mine.shape[1])
    coadd[0, 0:EDGE] = edges[0:EDGE]
    coadd[0, height - EDGE : height] = edges[EDGE : 2 * EDGE]
    taps[...] = jnp.zeros_like(taps)
    taps[0:1, 0:TAPS] = row_taps[...]
    taps[8:9, 0:TAPS] = col_taps[...]
    row, col = square_masks()
    near = jnp.abs(row - col) <= HALF
    square = around_matrix(taps[0:1, :])
    row_h, row_l = split2(jnp.where(near, square, 0.0))
    far = jnp.where(near, 0.0, square)
    far = pltpu.roll(jnp.concatenate([far[:EDGE], far[height - EDGE :]], axis=0), EDGE, 1)
    edge_m[...] = jnp.concatenate(split2(far), axis=0)
    matrix = col_matrix(taps[8:9, :])
    col_m[...] = matrix
    high, low = split2(coadd[0])
    smeared = jnp.dot(
        jnp.concatenate([row_h, row_l], axis=1),
        jnp.concatenate([high, high], axis=0),
        preferred_element_type=F32,
    ) + jnp.dot(row_h, low, preferred_element_type=F32)
    part[0:EDGE] = smeared[:EDGE]
    part[EDGE : 2 * EDGE] = smeared[height - EDGE :]
    filtered = col_conv(smeared[EDGE : height - EDGE], matrix)
    squares = filtered * filtered
    energy[...] = squares
    power[...] = lane_sums(squares)


def edge_psf_kernel(first, second, part, edge_m, col_m, inner, inner_power, energy, power, send):
    before, after = at_ends(first[...], second[...])
    window = jnp.concatenate([before, after], axis=0)
    both = jnp.dot(edge_m[:, 0 : 2 * EDGE], window, preferred_element_type=F32)
    filtered = col_conv(part[...] + (both[: 2 * EDGE] + both[2 * EDGE :]), col_m[...])
    squares = filtered * filtered
    energy[...] = squares
    total = inner_power[...] + lane_sums(squares)
    power[...] = total
    others, rows, width = send.shape
    half = rows - EDGE - 8
    own, core = lax.axis_index("band"), lax.axis_index("exp")
    for k in range(others):
        band = lax.rem(own + k + 1, others + 1)
        lanes = pl.ds(pl.multiple_of(band * width, width), width)
        send[k, 0:EDGE] = energy[pl.ds(pl.multiple_of(core * EDGE, EDGE), EDGE), lanes]
        send[k, EDGE : EDGE + half] = inner[pl.ds(pl.multiple_of(core * half, half), half), lanes]
        for n in range(width // LANES):
            send[k, EDGE + half : rows, n * LANES : (n + 1) * LANES] = total


def final_kernel(pixels, edges, inner, *refs):
    others = (len(refs) - 2) // 2
    mine, theirs, sums, detection = refs[:others], refs[others : 2 * others], refs[-2], refs[-1]
    height, width = detection.shape
    half = inner.shape[0] // 2
    lanes = pl.ds(pl.multiple_of(lax.axis_index("band") * width, width), width)
    scales = [1.0 / (jnp.sum(sums[i]) / pixels + EPSILON) for i in range(others + 1)]
    core = lax.axis_index("exp")
    for place, parts in ((core, mine), (1 - core, theirs)):
        for own, rows, to, start in (
            (edges, EDGE, place * (height - EDGE), 0),
            (inner, half, EDGE + place * half, EDGE),
        ):
            total = own[pl.ds(pl.multiple_of(place * rows, rows), rows), lanes] * scales[0]
            for i in range(others):
                total = total + parts[i][start : start + rows, :] * scales[i + 1]
            detection[pl.ds(pl.multiple_of(to, EDGE), rows), :] = total


def vmem(shape, dtype=F32):
    return jax.ShapeDtypeStruct(shape, dtype)


VMEM = pl.BlockSpec(memory_space=pltpu.VMEM)
SMEM = pl.BlockSpec(memory_space=pltpu.SMEM)
HBM = pl.BlockSpec(memory_space=pltpu.HBM)
PARAMS = pltpu.CompilerParams(vmem_limit_bytes=24 * MIB)


def paired(value, start):
    strips, cores = lax.axis_size("sky"), lax.axis_size("exp")
    partner = {}
    for i in range(start, strips - 1, 2):
        partner[i], partner[i + 1] = i + 1, i
    pairs = []
    for strip in range(strips):
        for core in range(cores):
            to = (partner[strip], core) if strip in partner else (strip, cores - 1 - core)
            pairs.append((strip * cores + core, to[0] * cores + to[1]))
    return lax.ppermute(value, ("sky", "exp"), pairs)


def flipped(value, axis, bits):
    return lax.ppermute(value, axis, [(i, i ^ bits) for i in range(lax.axis_size(axis))])


def turned(value, axis, step):
    size = lax.axis_size(axis)
    return lax.ppermute(value, axis, [(i, (i + step) % size) for i in range(size)])


def on_device(images, valid_mask, row_kernel, col_kernel, exp_group, zero_point, psf_row, psf_col):
    _, visits, height, cols = images.shape
    inner = height - 2 * EDGE
    bands = lax.axis_size("band")
    strips = lax.axis_size("sky")
    even = lax.rem(lax.axis_index("sky"), 2) == 0
    far = jnp.where(even, height - EDGE, 0)
    first = paired(lax.dynamic_slice_in_dim(images[0], far, EDGE, 1), 0)
    second = paired(lax.dynamic_slice_in_dim(images[0], height - EDGE - far, EDGE, 1), 1)

    lists = 2 * REJECT + 2
    early = inner // 16 * 8
    early_lists, late_lists, part, edge_m, col_m, edge_mask = pl.pallas_call(
        inner_kernel,
        in_specs=[HBM] * 6,
        out_specs=[VMEM] * 6,
        out_shape=[
            vmem((lists, early, cols)),
            vmem((lists, inner - early, cols)),
            vmem((visits, 2 * EDGE, cols)),
            vmem((visits, 4 * EDGE, LANES), BF16),
            vmem((visits, 2 * LANES, 2 * LANES), BF16),
            vmem((visits, 2 * EDGE, cols), jnp.int32),
        ],
        scratch_shapes=[
            pltpu.SMEM((1, visits), jnp.int32),
            pltpu.SMEM(zero_point.shape, F32),
            pltpu.VMEM((visits, 1, TAPS), F32),
            pltpu.VMEM((visits, 1, TAPS), F32),
            pltpu.VMEM((visits, height, cols), BF16),
            pltpu.VMEM((visits, height, cols), jnp.int32),
            pltpu.VMEM((16 * UNROLL, LANES), F32),
            pltpu.VMEM((visits, LANES, 2 * LANES), BF16),
            pltpu.VMEM((visits, inner, cols), F32),
            pltpu.VMEM((visits, inner, cols), F32),
            pltpu.VMEM((visits, inner, cols), F32),
            pltpu.VMEM((inner, cols), F32),
            pltpu.VMEM((inner, cols), jnp.int32),
            pltpu.SemaphoreType.DMA((4,)),
            pltpu.SemaphoreType.DMA((2,)),
            pltpu.SemaphoreType.DMA((2,)),
        ],
        compiler_params=PARAMS,
        cost_estimate=pl.CostEstimate(
            flops=visits * height * cols * 4096,
            bytes_accessed=visits * height * cols * 6,
            transcendentals=0,
        ),
        name="inner_visits",
    )(
        *(
            pltpu.with_memory_space_constraint(value, pltpu.HBM)
            for value in (
                exp_group,
                zero_point,
                images,
                valid_mask,
                row_kernel.transpose(1, 0, 2),
                col_kernel.transpose(1, 0, 2),
            )
        )
    )
    swap = [(0, 1), (1, 0)]
    held, first, second = lax.optimization_barrier((early_lists, first, second))
    early_other = lax.ppermute(held, "exp", swap)
    edge_lists = pl.pallas_call(
        edge_kernel,
        in_specs=[VMEM] * 6,
        out_specs=VMEM,
        out_shape=vmem((lists, 2 * EDGE, cols)),
        scratch_shapes=[pltpu.VMEM((visits, 2 * EDGE, cols), F32)] * 3
        + [pltpu.VMEM((2 * EDGE, cols), F32), pltpu.VMEM((2 * EDGE, cols), jnp.int32)],
        compiler_params=PARAMS,
        cost_estimate=pl.CostEstimate(
            flops=visits * height * cols * 6144, bytes_accessed=visits * cols * 256, transcendentals=0
        ),
        name="edge_visits",
    )(first, second, part, edge_m, col_m, edge_mask)
    edge_other = lax.ppermute(edge_lists, "exp", swap)

    held, _ = lax.optimization_barrier((late_lists, edge_other))
    late_other = lax.ppermute(held, "exp", swap)

    edges, send_first, send_second = pl.pallas_call(
        edge_merge_kernel,
        in_specs=[VMEM] * 2,
        out_specs=[VMEM] * 3,
        out_shape=[vmem((2 * EDGE, cols)), vmem((EDGE, cols), BF16), vmem((EDGE, cols), BF16)],
        compiler_params=PARAMS,
        name="edge_merge",
    )(edge_lists, edge_other)
    coadd_first = paired(send_first, 0)
    coadd_second = paired(send_second, 1)
    coadd_image, inner_energy, inner_power, psf_part, psf_edge_m, psf_col_m = pl.pallas_call(
        inner_psf_kernel,
        in_specs=[VMEM] * 7,
        out_specs=[VMEM] * 6,
        out_shape=[
            vmem((1, height, cols)),
            vmem((inner, cols)),
            vmem((8, LANES)),
            vmem((2 * EDGE, cols)),
            vmem((4 * EDGE, LANES), BF16),
            vmem((2 * LANES, 2 * LANES), BF16),
        ],
        scratch_shapes=[pltpu.VMEM((16, LANES), F32)],
        compiler_params=PARAMS,
        name="inner_psf",
    )(early_lists, early_other, late_lists, late_other, edges, psf_row, psf_col)

    width = cols // bands
    edge_energy, power, send = pl.pallas_call(
        edge_psf_kernel,
        in_specs=[VMEM] * 7,
        out_specs=[VMEM] * 3,
        out_shape=[
            vmem((2 * EDGE, cols)),
            vmem((8, LANES)),
            vmem((bands - 1, height // 2 + 8, width)),
        ],
        compiler_params=PARAMS,
        name="edge_psf",
    )(coadd_first, coadd_second, psf_part, psf_edge_m, psf_col_m, inner_energy, inner_power)

    mine = [turned(send[k - 1], "band", k) for k in range(1, bands)]
    held = [part[height // 2 :, :LANES] for part in mine]
    if strips == 4 and bands == 2 and lax.axis_size("exp") == 2:
        first_core = lax.axis_index("exp") == 0
        total = 0.0
        for bits in range(1, strips):
            pairs = []
            for strip in range(strips):
                for core in range(2):
                    for band in range(2):
                        to = (strip ^ bits, core, band ^ core)
                        pairs.append((4 * strip + 2 * core + band, 4 * to[0] + 2 * to[1] + to[2]))
            total = total + lax.ppermute(power, ("sky", "exp", "band"), pairs)
        total = total + jnp.where(first_core, power, held[0])
        theirs = [lax.ppermute(mine[0], "exp", swap)]
        total, _ = lax.optimization_barrier((total, theirs[0]))
        other = lax.ppermute(total, "exp", swap)
        sums = jnp.where(first_core, jnp.stack([total, other]), jnp.stack([other, total]))
    else:
        theirs = [lax.ppermute(part, "exp", swap) for part in mine]
        sums = lax.psum(jnp.stack([power] + held), "sky")
    pixels = height * strips * cols
    detection = pl.pallas_call(
        functools.partial(final_kernel, pixels),
        in_specs=[VMEM] * (2 * bands + 1),
        out_specs=VMEM,
        out_shape=vmem((height, width)),
        compiler_params=PARAMS,
        name="detection",
    )(edge_energy, inner_energy, *mine, *theirs, sums)
    return coadd_image, detection


def solution(mesh):
    placed = (
        P("band", "exp", ("patch", "sky"), None),
        P("band", "exp", ("patch", "sky"), None),
        P("band", "exp", None),
        P("band", "exp", None),
        P("band", "exp"),
        P("band", None),
        P("band", None),
        P("band", None),
    )
    return jax.shard_map(
        on_device,
        mesh=mesh,
        in_specs=placed,
        out_specs=(P("band", ("patch", "sky"), None), P(("patch", "sky"), "band")),
        check_vma=False,
    )
```

```python
import functools

import jax
import jax.numpy as jnp
from jax import lax
from jax.experimental import pallas as pl
from jax.experimental.pallas import tpu as pltpu
from jax.sharding import PartitionSpec as P

HALF = 15
REJECT = 4
TAPS = 31
EDGE = 16
LANES = 128
SENTINEL = 1e30
EPSILON = 1e-05
F32 = jnp.float32
BF16 = jnp.bfloat16
MIB = 1024 * 1024
UNROLL = 2


def split2(value):
    high = value.astype(BF16)
    return high, (value - high.astype(F32)).astype(BF16)


def band_rows(taps, rows):
    return pltpu.roll(
        jnp.broadcast_to(pltpu.roll(taps, 1, 1), (rows, LANES)), 0, 1, stride=1, stride_axis=0
    )


def around_matrix(taps):
    base = pltpu.roll(taps, LANES - HALF, 1)
    return pltpu.roll(jnp.broadcast_to(base, (LANES, LANES)), 0, 1, stride=1, stride_axis=0)


def square_masks():
    row = lax.broadcasted_iota(jnp.int32, (LANES, LANES), 0)
    col = lax.broadcasted_iota(jnp.int32, (LANES, LANES), 1)
    return row, col


def col_matrix(taps):
    return jnp.concatenate(split2(row_matrix(taps)), axis=0)


def row_matrix(taps):
    square = band_rows(taps, LANES)
    row, col = square_masks()
    return jnp.concatenate(
        [jnp.where(col > row, square, 0.0), jnp.where(col < row, square, 0.0)], axis=1
    )


def col_conv(value, matrix):
    rows, cols = value.shape
    tiles = cols // LANES
    turned = pltpu.roll(value, EDGE, 1)
    first = turned[:, :LANES]
    lane = lax.broadcasted_iota(jnp.int32, (rows, LANES), 1)
    wide = jnp.concatenate(
        [jnp.where(lane < EDGE, 0.0, first), turned[:, LANES:], jnp.where(lane < EDGE, first, 0.0)],
        axis=1,
    )
    parts = [
        part[:, n * LANES : (n + 2) * LANES] for part in split2(wide) for n in range(tiles)
    ]
    product = lax.dot_general(
        jnp.concatenate(parts, axis=0),
        matrix,
        (((1,), (1,)), ((), ())),
        preferred_element_type=F32,
    )

    def piece(n, side):
        return product[n * rows : (n + 1) * rows, side * LANES : (side + 1) * LANES]

    return jnp.concatenate(
        [piece(n, 0) + (piece(n, 1) + piece(tiles + n, 0)) for n in range(tiles)], axis=1
    )


def ordered(values, pairs, first, second):
    values = list(values)
    for i, j in pairs:
        values[i], values[j] = first(values[i], values[j]), second(values[i], values[j])
    return values


def foremost(groups, first, second):
    best = None
    while groups:
        group, groups = groups[0], groups[1:]
        if len(group) == 2 and groups and len(groups[0]) == 2:
            group, groups = [*group, *groups[0]], groups[1:]
            group = ordered(group, ((0, 2), (1, 3), (1, 2)), first, second)
        if best is None:
            best = group
        elif len(best) < REJECT:
            best = best + group
            pairs = [(j, j + 1) for i in range(len(best)) for j in range(len(best) - 1 - i)]
            best = ordered(best, pairs, first, second)[:REJECT]
        else:
            best = list(best)
            for i, value in enumerate(group):
                best[REJECT - 1 - i] = first(best[REJECT - 1 - i], value)
            best = ordered(best, ((0, 2), (1, 3), (0, 1), (2, 3)), first, second)
    return best


def hold(visit, results, masks, upper, lower, totals, counts):
    masks = [mask for mask in masks]
    usable = [mask == 1 for mask in masks]
    tops = [jnp.where(use, value, -SENTINEL) for use, value in zip(usable, results)]
    ends = [jnp.where(use, value, SENTINEL) for use, value in zip(usable, results)]
    if len(results) == 2:
        tops = ordered(tops, ((0, 1),), jnp.maximum, jnp.minimum)
        ends = ordered(ends, ((0, 1),), jnp.minimum, jnp.maximum)
    for i in range(len(results)):
        upper[visit + i] = tops[i]
        lower[visit + i] = ends[i]
    totals[...] += sum(jnp.where(use, value, 0.0) for use, value in zip(usable, results))
    counts[...] += sum(masks)


def sort_visits(at_once, upper, lower, totals, counts, start, lists):
    visits, _, cols = upper.shape
    rows = lists.shape[1]
    width = 2 * LANES

    def body(step, carry):
        at = pl.ds(pl.multiple_of(step * 8, 8), 8)
        source = pl.ds(pl.multiple_of(step * 8 + start, 8), 8)
        for left in range(0, cols, width):
            lanes = pl.ds(left, width)
            for place, values, first, second in (
                (0, upper, jnp.maximum, jnp.minimum),
                (REJECT, lower, jnp.minimum, jnp.maximum),
            ):
                groups = [
                    [values[v + i, source, lanes] for i in range(at_once)]
                    for v in range(0, visits, at_once)
                ]
                for i, value in enumerate(foremost(groups, first, second)):
                    lists[place + i, at, lanes] = value
            lists[2 * REJECT, at, lanes] = totals[source, lanes]
            lists[2 * REJECT + 1, at, lanes] = counts[source, lanes].astype(F32)
        return carry

    lax.fori_loop(0, rows // 8, body, 0)


def inner_kernel(
    groups_h,
    points_h,
    images_h,
    mask_h,
    row_taps_h,
    col_taps_h,
    early_lists,
    late_lists,
    part,
    edge_m,
    col_m,
    edge_mask,
    groups,
    points,
    row_taps,
    col_taps,
    images,
    mask,
    taps,
    row_m,
    values,
    upper,
    lower,
    totals,
    counts,
    small_sems,
    image_sems,
    mask_sems,
):
    visits, height, _ = images.shape
    small = [
        pltpu.make_async_copy(source, target, small_sems.at[i])
        for i, (source, target) in enumerate(
            ((groups_h, groups), (points_h, points), (row_taps_h, row_taps), (col_taps_h, col_taps))
        )
    ]

    middle = visits // 2 // UNROLL * UNROLL if visits % UNROLL == 0 else visits // 2

    def image_copy(i):
        at = pl.ds(0, middle) if i == 0 else pl.ds(middle, visits - middle)
        return pltpu.make_async_copy(images_h.at[0, at], images.at[at], image_sems.at[i])

    def mask_copy(i):
        at = pl.ds(0, middle) if i == 0 else pl.ds(middle, visits - middle)
        return pltpu.make_async_copy(mask_h.at[0, at], mask.at[at], mask_sems.at[i])

    for copy in small:
        copy.start()
    for i in range(2):
        image_copy(i).start()
        mask_copy(i).start()
    taps[...] = jnp.zeros_like(taps)
    totals[...] = jnp.zeros_like(totals)
    counts[...] = jnp.zeros_like(counts)
    row, col = square_masks()
    near = jnp.abs(row - col) <= HALF
    for copy in small:
        copy.wait()
    def build(v, slot):
        taps[slot : slot + 1, 0:TAPS] = row_taps[v]
        taps[slot + 8 : slot + 9, 0:TAPS] = col_taps[v]
        scale = points[0, groups[0, v]]
        square = around_matrix(taps[slot : slot + 1, :])
        row_m[v] = jnp.concatenate(split2(jnp.where(near, square, 0.0)), axis=1)
        far = jnp.where(near, 0.0, square)
        far = pltpu.roll(jnp.concatenate([far[:EDGE], far[height - EDGE :]], axis=0), EDGE, 1)
        edge_m[v] = jnp.concatenate(split2(far), axis=0)
        col_m[v] = col_matrix(taps[slot + 8 : slot + 9, :] * scale)

    def smear(v):
        image = images[v]
        smeared = jnp.dot(
            row_m[v], jnp.concatenate([image, image], axis=0), preferred_element_type=F32
        )
        values[v] = smeared[EDGE : height - EDGE]
        part[v, 0:EDGE] = smeared[:EDGE]
        part[v, EDGE : 2 * EDGE] = smeared[height - EDGE :]

    def convolve(v, number):
        results = [col_conv(values[v + i], col_m[v + i]) for i in range(number)]
        masks = [mask[v + i, EDGE : height - EDGE] for i in range(number)]
        hold(v, results, masks, upper, lower, totals, counts)
        for i in range(number):
            edge_mask[v + i, 0:EDGE] = mask[v + i, 0:EDGE]
            edge_mask[v + i, EDGE : 2 * EDGE] = mask[v + i, height - EDGE :]

    at_once = UNROLL if visits % UNROLL == 0 else 1
    steps = visits // at_once

    def work(step, most=None):
        convolve(step * at_once, at_once)
        for i in range(at_once):
            if most is None or most >= 1:
                smear((step + 1) * at_once + i)
        for i in range(at_once):
            if most is None or most >= 2:
                build((step + 2) * at_once + i, 16 * i)

    for step in range(min(2, steps)):
        for i in range(at_once):
            build(step * at_once + i, 16 * i)
    image_copy(0).wait()
    mask_copy(0).wait()
    for i in range(at_once):
        smear(i)
    ready = max(min(middle // at_once - 1, steps - 2), 0)

    def body(step, carry):
        work(step)
        return carry

    lax.fori_loop(0, ready, body, 0)
    image_copy(1).wait()
    mask_copy(1).wait()
    lax.fori_loop(ready, steps - 2, body, 0)
    for step in range(max(steps - 2, 0), steps):
        work(step, steps - 1 - step)
    held = (at_once, upper, lower, totals, counts)
    sort_visits(*held, 0, early_lists)
    sort_visits(*held, early_lists.shape[1], late_lists)


def at_ends(first, second):
    strip = lax.axis_index("sky")
    even = lax.rem(strip, 2) == 0
    top, bottom = strip == 0, strip == lax.axis_size("sky") - 1
    above, below = jnp.where(even, second, first), jnp.where(even, first, second)
    return (
        jnp.where(top, jnp.zeros_like(above), above),
        jnp.where(bottom, jnp.zeros_like(below), below),
    )


def edge_kernel(
    first, second, part, edge_m, col_m, edge_mask, lists, values, upper, lower, totals, counts
):
    visits, _, cols = values.shape
    for visit in range(visits):
        before, after = at_ends(first[visit], second[visit])
        window = jnp.concatenate([before, after], axis=0)
        both = jnp.dot(edge_m[visit, :, 0 : 2 * EDGE], window, preferred_element_type=F32)
        values[visit] = part[visit] + (both[: 2 * EDGE] + both[2 * EDGE :])
    at_once = UNROLL if visits % UNROLL == 0 else 1
    totals[...] = jnp.zeros_like(totals)
    counts[...] = jnp.zeros_like(counts)
    for visit in range(0, visits, at_once):
        results = [col_conv(values[visit + i], col_m[visit + i]) for i in range(at_once)]
        masks = [edge_mask[visit + i] for i in range(at_once)]
        hold(visit, results, masks, upper, lower, totals, counts)
    sort_visits(at_once, upper, lower, totals, counts, 0, lists)


def merge(mine, other, coadd, start):
    def body(step, carry):
        at = pl.ds(pl.multiple_of(step * 8, 8), 8)
        upper, lower = 0.0, 0.0
        for i in range(REJECT):
            j = REJECT - 1 - i
            upper = upper + jnp.maximum(mine[i, at, :], other[j, at, :])
            lower = lower + jnp.minimum(mine[REJECT + i, at, :], other[REJECT + j, at, :])
        total = mine[2 * REJECT, at, :] + other[2 * REJECT, at, :]
        count = mine[2 * REJECT + 1, at, :] + other[2 * REJECT + 1, at, :]
        coadd[pl.ds(pl.multiple_of(step * 8 + start, 8), 8), :] = (total - upper - lower) / (
            count - 2 * REJECT
        )
        return carry

    lax.fori_loop(0, mine.shape[1] // 8, body, 0)


def edge_merge_kernel(mine, other, coadd, send_first, send_second):
    merge(mine, other, coadd, 0)
    even = lax.rem(lax.axis_index("sky"), 2) == 0
    top, bottom = coadd[0:EDGE], coadd[EDGE : 2 * EDGE]
    send_first[...] = jnp.where(even, bottom, top).astype(BF16)
    send_second[...] = jnp.where(even, top, bottom).astype(BF16)


def lane_sums(squares):
    rows, cols = squares.shape
    part = jnp.sum(squares.reshape(rows // 8, 8, cols), axis=0)
    return sum(part[:, n * LANES : (n + 1) * LANES] for n in range(cols // LANES))


def inner_psf_kernel(
    early_mine,
    early_other,
    late_mine,
    late_other,
    edges,
    row_taps,
    col_taps,
    coadd,
    energy,
    power,
    part,
    edge_m,
    col_m,
    taps,
):
    height = coadd.shape[1]
    merge(early_mine, early_other, coadd.at[0], EDGE)
    merge(late_mine, late_other, coadd.at[0], EDGE + early_mine.shape[1])
    coadd[0, 0:EDGE] = edges[0:EDGE]
    coadd[0, height - EDGE : height] = edges[EDGE : 2 * EDGE]
    taps[...] = jnp.zeros_like(taps)
    taps[0:1, 0:TAPS] = row_taps[...]
    taps[8:9, 0:TAPS] = col_taps[...]
    row, col = square_masks()
    near = jnp.abs(row - col) <= HALF
    square = around_matrix(taps[0:1, :])
    row_h, row_l = split2(jnp.where(near, square, 0.0))
    far = jnp.where(near, 0.0, square)
    far = pltpu.roll(jnp.concatenate([far[:EDGE], far[height - EDGE :]], axis=0), EDGE, 1)
    edge_m[...] = jnp.concatenate(split2(far), axis=0)
    matrix = col_matrix(taps[8:9, :])
    col_m[...] = matrix
    high, low = split2(coadd[0])
    smeared = jnp.dot(
        jnp.concatenate([row_h, row_l], axis=1),
        jnp.concatenate([high, high], axis=0),
        preferred_element_type=F32,
    ) + jnp.dot(row_h, low, preferred_element_type=F32)
    part[0:EDGE] = smeared[:EDGE]
    part[EDGE : 2 * EDGE] = smeared[height - EDGE :]
    filtered = col_conv(smeared[EDGE : height - EDGE], matrix)
    squares = filtered * filtered
    energy[...] = squares
    power[...] = lane_sums(squares)


def edge_psf_kernel(first, second, part, edge_m, col_m, inner, inner_power, energy, power, send):
    before, after = at_ends(first[...], second[...])
    window = jnp.concatenate([before, after], axis=0)
    both = jnp.dot(edge_m[:, 0 : 2 * EDGE], window, preferred_element_type=F32)
    filtered = col_conv(part[...] + (both[: 2 * EDGE] + both[2 * EDGE :]), col_m[...])
    squares = filtered * filtered
    energy[...] = squares
    total = inner_power[...] + lane_sums(squares)
    power[...] = total
    others, rows, width = send.shape
    half = rows - EDGE - 8
    own, core = lax.axis_index("band"), lax.axis_index("exp")
    for k in range(others):
        band = lax.rem(own + k + 1, others + 1)
        lanes = pl.ds(pl.multiple_of(band * width, width), width)
        send[k, 0:EDGE] = energy[pl.ds(pl.multiple_of(core * EDGE, EDGE), EDGE), lanes]
        send[k, EDGE : EDGE + half] = inner[pl.ds(pl.multiple_of(core * half, half), half), lanes]
        for n in range(width // LANES):
            send[k, EDGE + half : rows, n * LANES : (n + 1) * LANES] = total


def final_kernel(pixels, edges, inner, *refs):
    others = (len(refs) - 2) // 2
    mine, theirs, sums, detection = refs[:others], refs[others : 2 * others], refs[-2], refs[-1]
    height, width = detection.shape
    half = inner.shape[0] // 2
    lanes = pl.ds(pl.multiple_of(lax.axis_index("band") * width, width), width)
    scales = []
    for i in range(others + 1):
        whole = jnp.sum(jnp.sum(sums[i], axis=0, keepdims=True), axis=1, keepdims=True)
        scales.append(1.0 / (whole / pixels + EPSILON))
    core = lax.axis_index("exp")
    for place, parts in ((core, mine), (1 - core, theirs)):
        for own, rows, to, start in (
            (edges, EDGE, place * (height - EDGE), 0),
            (inner, half, EDGE + place * half, EDGE),
        ):
            total = own[pl.ds(pl.multiple_of(place * rows, rows), rows), lanes] * scales[0]
            for i in range(others):
                total = total + parts[i][start : start + rows, :] * scales[i + 1]
            detection[pl.ds(pl.multiple_of(to, EDGE), rows), :] = total


def vmem(shape, dtype=F32):
    return jax.ShapeDtypeStruct(shape, dtype)


VMEM = pl.BlockSpec(memory_space=pltpu.VMEM)
SMEM = pl.BlockSpec(memory_space=pltpu.SMEM)
HBM = pl.BlockSpec(memory_space=pltpu.HBM)
PARAMS = pltpu.CompilerParams(vmem_limit_bytes=24 * MIB)


def paired(value, start):
    strips, cores = lax.axis_size("sky"), lax.axis_size("exp")
    partner = {}
    for i in range(start, strips - 1, 2):
        partner[i], partner[i + 1] = i + 1, i
    pairs = []
    for strip in range(strips):
        for core in range(cores):
            to = (partner[strip], core) if strip in partner else (strip, cores - 1 - core)
            pairs.append((strip * cores + core, to[0] * cores + to[1]))
    return lax.ppermute(value, ("sky", "exp"), pairs)


def flipped(value, axis, bits):
    return lax.ppermute(value, axis, [(i, i ^ bits) for i in range(lax.axis_size(axis))])


def turned(value, axis, step):
    size = lax.axis_size(axis)
    return lax.ppermute(value, axis, [(i, (i + step) % size) for i in range(size)])


def on_device(images, valid_mask, row_kernel, col_kernel, exp_group, zero_point, psf_row, psf_col):
    _, visits, height, cols = images.shape
    inner = height - 2 * EDGE
    bands = lax.axis_size("band")
    strips = lax.axis_size("sky")
    even = lax.rem(lax.axis_index("sky"), 2) == 0
    far = jnp.where(even, height - EDGE, 0)
    first = paired(lax.dynamic_slice_in_dim(images[0], far, EDGE, 1), 0)
    second = paired(lax.dynamic_slice_in_dim(images[0], height - EDGE - far, EDGE, 1), 1)

    lists = 2 * REJECT + 2
    early = inner // 16 * 8
    early_lists, late_lists, part, edge_m, col_m, edge_mask = pl.pallas_call(
        inner_kernel,
        in_specs=[HBM] * 6,
        out_specs=[VMEM] * 6,
        out_shape=[
            vmem((lists, early, cols)),
            vmem((lists, inner - early, cols)),
            vmem((visits, 2 * EDGE, cols)),
            vmem((visits, 4 * EDGE, LANES), BF16),
            vmem((visits, 2 * LANES, 2 * LANES), BF16),
            vmem((visits, 2 * EDGE, cols), jnp.int32),
        ],
        scratch_shapes=[
            pltpu.SMEM((1, visits), jnp.int32),
            pltpu.SMEM(zero_point.shape, F32),
            pltpu.VMEM((visits, 1, TAPS), F32),
            pltpu.VMEM((visits, 1, TAPS), F32),
            pltpu.VMEM((visits, height, cols), BF16),
            pltpu.VMEM((visits, height, cols), jnp.int32),
            pltpu.VMEM((16 * UNROLL, LANES), F32),
            pltpu.VMEM((visits, LANES, 2 * LANES), BF16),
            pltpu.VMEM((visits, inner, cols), F32),
            pltpu.VMEM((visits, inner, cols), F32),
            pltpu.VMEM((visits, inner, cols), F32),
            pltpu.VMEM((inner, cols), F32),
            pltpu.VMEM((inner, cols), jnp.int32),
            pltpu.SemaphoreType.DMA((4,)),
            pltpu.SemaphoreType.DMA((2,)),
            pltpu.SemaphoreType.DMA((2,)),
        ],
        compiler_params=PARAMS,
        cost_estimate=pl.CostEstimate(
            flops=visits * height * cols * 4096,
            bytes_accessed=visits * height * cols * 6,
            transcendentals=0,
        ),
        name="inner_visits",
    )(
        *(
            pltpu.with_memory_space_constraint(value, pltpu.HBM)
            for value in (
                exp_group,
                zero_point,
                images,
                valid_mask,
                row_kernel.transpose(1, 0, 2),
                col_kernel.transpose(1, 0, 2),
            )
        )
    )
    swap = [(0, 1), (1, 0)]
    held, first, second = lax.optimization_barrier((early_lists, first, second))
    early_other = lax.ppermute(held, "exp", swap)
    edge_lists = pl.pallas_call(
        edge_kernel,
        in_specs=[VMEM] * 6,
        out_specs=VMEM,
        out_shape=vmem((lists, 2 * EDGE, cols)),
        scratch_shapes=[pltpu.VMEM((visits, 2 * EDGE, cols), F32)] * 3
        + [pltpu.VMEM((2 * EDGE, cols), F32), pltpu.VMEM((2 * EDGE, cols), jnp.int32)],
        compiler_params=PARAMS,
        cost_estimate=pl.CostEstimate(
            flops=visits * height * cols * 6144, bytes_accessed=visits * cols * 256, transcendentals=0
        ),
        name="edge_visits",
    )(first, second, part, edge_m, col_m, edge_mask)
    edge_other = lax.ppermute(edge_lists, "exp", swap)

    held, _ = lax.optimization_barrier((late_lists, edge_other))
    late_other = lax.ppermute(held, "exp", swap)

    edges, send_first, send_second = pl.pallas_call(
        edge_merge_kernel,
        in_specs=[VMEM] * 2,
        out_specs=[VMEM] * 3,
        out_shape=[vmem((2 * EDGE, cols)), vmem((EDGE, cols), BF16), vmem((EDGE, cols), BF16)],
        compiler_params=PARAMS,
        name="edge_merge",
    )(edge_lists, edge_other)
    coadd_first = paired(send_first, 0)
    coadd_second = paired(send_second, 1)
    coadd_image, inner_energy, inner_power, psf_part, psf_edge_m, psf_col_m = pl.pallas_call(
        inner_psf_kernel,
        in_specs=[VMEM] * 7,
        out_specs=[VMEM] * 6,
        out_shape=[
            vmem((1, height, cols)),
            vmem((inner, cols)),
            vmem((8, LANES)),
            vmem((2 * EDGE, cols)),
            vmem((4 * EDGE, LANES), BF16),
            vmem((2 * LANES, 2 * LANES), BF16),
        ],
        scratch_shapes=[pltpu.VMEM((16, LANES), F32)],
        compiler_params=PARAMS,
        name="inner_psf",
    )(early_lists, early_other, late_lists, late_other, edges, psf_row, psf_col)

    width = cols // bands
    edge_energy, power, send = pl.pallas_call(
        edge_psf_kernel,
        in_specs=[VMEM] * 7,
        out_specs=[VMEM] * 3,
        out_shape=[
            vmem((2 * EDGE, cols)),
            vmem((8, LANES)),
            vmem((bands - 1, height // 2 + 8, width)),
        ],
        compiler_params=PARAMS,
        name="edge_psf",
    )(coadd_first, coadd_second, psf_part, psf_edge_m, psf_col_m, inner_energy, inner_power)

    mine = [turned(send[k - 1], "band", k) for k in range(1, bands)]
    held = [part[height // 2 :, :LANES] for part in mine]
    if strips == 4 and bands == 2 and lax.axis_size("exp") == 2:
        first_core = lax.axis_index("exp") == 0
        total = 0.0
        for bits in range(1, strips):
            pairs = []
            for strip in range(strips):
                for core in range(2):
                    for band in range(2):
                        to = (strip ^ bits, core, band ^ core)
                        pairs.append((4 * strip + 2 * core + band, 4 * to[0] + 2 * to[1] + to[2]))
            total = total + lax.ppermute(power, ("sky", "exp", "band"), pairs)
        total = total + jnp.where(first_core, power, held[0])
        theirs = [lax.ppermute(mine[0], "exp", swap)]
        total, _ = lax.optimization_barrier((total, theirs[0]))
        other = lax.ppermute(total, "exp", swap)
        sums = jnp.where(first_core, jnp.stack([total, other]), jnp.stack([other, total]))
    else:
        theirs = [lax.ppermute(part, "exp", swap) for part in mine]
        sums = lax.psum(jnp.stack([power] + held), "sky")
    pixels = height * strips * cols
    detection = pl.pallas_call(
        functools.partial(final_kernel, pixels),
        in_specs=[VMEM] * (2 * bands + 1),
        out_specs=VMEM,
        out_shape=vmem((height, width)),
        compiler_params=PARAMS,
        name="detection",
    )(edge_energy, inner_energy, *mine, *theirs, sums)
    return coadd_image, detection


def solution(mesh):
    placed = (
        P("band", "exp", ("patch", "sky"), None),
        P("band", "exp", ("patch", "sky"), None),
        P("band", "exp", None),
        P("band", "exp", None),
        P("band", "exp"),
        P("band", None),
        P("band", None),
        P("band", None),
    )
    return jax.shard_map(
        on_device,
        mesh=mesh,
        in_specs=placed,
        out_specs=(P("band", ("patch", "sky"), None), P(("patch", "sky"), "band")),
        check_vma=False,
    )
```

```python
import functools

import jax
import jax.numpy as jnp
from jax import lax
from jax.experimental import pallas as pl
from jax.experimental.pallas import tpu as pltpu
from jax.sharding import PartitionSpec as P

HALF = 15
REJECT = 4
TAPS = 31
EDGE = 16
LANES = 128
SENTINEL = 1e30
EPSILON = 1e-05
F32 = jnp.float32
BF16 = jnp.bfloat16
MIB = 1024 * 1024
UNROLL = 2


def split2(value):
    high = value.astype(BF16)
    return high, (value - high.astype(F32)).astype(BF16)


def band_rows(taps, rows):
    return pltpu.roll(
        jnp.broadcast_to(pltpu.roll(taps, 1, 1), (rows, LANES)), 0, 1, stride=1, stride_axis=0
    )


def around_matrix(taps):
    base = pltpu.roll(taps, LANES - HALF, 1)
    return pltpu.roll(jnp.broadcast_to(base, (LANES, LANES)), 0, 1, stride=1, stride_axis=0)


def square_masks():
    row = lax.broadcasted_iota(jnp.int32, (LANES, LANES), 0)
    col = lax.broadcasted_iota(jnp.int32, (LANES, LANES), 1)
    return row, col


def col_matrix(taps):
    return jnp.concatenate(split2(row_matrix(taps)), axis=0)


def row_matrix(taps):
    square = band_rows(taps, LANES)
    row, col = square_masks()
    return jnp.concatenate(
        [jnp.where(col > row, square, 0.0), jnp.where(col < row, square, 0.0)], axis=1
    )


def col_conv(value, matrix):
    rows, cols = value.shape
    tiles = cols // LANES
    turned = pltpu.roll(value, EDGE, 1)
    first = turned[:, :LANES]
    lane = lax.broadcasted_iota(jnp.int32, (rows, LANES), 1)
    wide = jnp.concatenate(
        [jnp.where(lane < EDGE, 0.0, first), turned[:, LANES:], jnp.where(lane < EDGE, first, 0.0)],
        axis=1,
    )
    parts = [
        part[:, n * LANES : (n + 2) * LANES] for part in split2(wide) for n in range(tiles)
    ]
    product = lax.dot_general(
        jnp.concatenate(parts, axis=0),
        matrix,
        (((1,), (1,)), ((), ())),
        preferred_element_type=F32,
    )

    def piece(n, side):
        return product[n * rows : (n + 1) * rows, side * LANES : (side + 1) * LANES]

    return jnp.concatenate(
        [piece(n, 0) + (piece(n, 1) + piece(tiles + n, 0)) for n in range(tiles)], axis=1
    )


def ordered(values, pairs, first, second):
    values = list(values)
    for i, j in pairs:
        values[i], values[j] = first(values[i], values[j]), second(values[i], values[j])
    return values


def foremost(groups, first, second):
    best = None
    while groups:
        group, groups = groups[0], groups[1:]
        if len(group) == 2 and groups and len(groups[0]) == 2:
            group, groups = [*group, *groups[0]], groups[1:]
            group = ordered(group, ((0, 2), (1, 3), (1, 2)), first, second)
        if best is None:
            best = group
        elif len(best) < REJECT:
            best = best + group
            pairs = [(j, j + 1) for i in range(len(best)) for j in range(len(best) - 1 - i)]
            best = ordered(best, pairs, first, second)[:REJECT]
        else:
            best = list(best)
            for i, value in enumerate(group):
                best[REJECT - 1 - i] = first(best[REJECT - 1 - i], value)
            best = ordered(best, ((0, 2), (1, 3), (0, 1), (2, 3)), first, second)
    return best


def hold(visit, results, masks, upper, lower, totals, counts):
    masks = [mask for mask in masks]
    usable = [mask == 1 for mask in masks]
    tops = [jnp.where(use, value, -SENTINEL) for use, value in zip(usable, results)]
    ends = [jnp.where(use, value, SENTINEL) for use, value in zip(usable, results)]
    if len(results) == 2:
        tops = ordered(tops, ((0, 1),), jnp.maximum, jnp.minimum)
        ends = ordered(ends, ((0, 1),), jnp.minimum, jnp.maximum)
    for i in range(len(results)):
        upper[visit + i] = tops[i]
        lower[visit + i] = ends[i]
    totals[...] += sum(jnp.where(use, value, 0.0) for use, value in zip(usable, results))
    counts[...] += sum(masks)


def sort_visits(at_once, upper, lower, totals, counts, start, lists):
    visits, _, cols = upper.shape
    rows = lists.shape[1]
    width = 2 * LANES

    def body(step, carry):
        at = pl.ds(pl.multiple_of(step * 8, 8), 8)
        source = pl.ds(pl.multiple_of(step * 8 + start, 8), 8)
        for left in range(0, cols, width):
            lanes = pl.ds(left, width)
            for place, values, first, second in (
                (0, upper, jnp.maximum, jnp.minimum),
                (REJECT, lower, jnp.minimum, jnp.maximum),
            ):
                groups = [
                    [values[v + i, source, lanes] for i in range(at_once)]
                    for v in range(0, visits, at_once)
                ]
                for i, value in enumerate(foremost(groups, first, second)):
                    lists[place + i, at, lanes] = value
            lists[2 * REJECT, at, lanes] = totals[source, lanes]
            lists[2 * REJECT + 1, at, lanes] = counts[source, lanes].astype(F32)
        return carry

    lax.fori_loop(0, rows // 8, body, 0)


def rim_kernel(images, first, second, sems):
    rows = first.shape[1]
    last = images.shape[2] - rows
    far = jnp.where(lax.rem(lax.axis_index("sky"), 2) == 0, last, 0)
    copies = [
        pltpu.make_async_copy(
            images.at[0, :, pl.ds(pl.multiple_of(start, EDGE), rows)], target, sems.at[i]
        )
        for i, (start, target) in enumerate(((far, first), (last - far, second)))
    ]
    for copy in copies:
        copy.start()
    for copy in copies:
        copy.wait()


def inner_kernel(
    groups_h,
    points_h,
    images_h,
    mask_h,
    row_taps_h,
    col_taps_h,
    early_lists,
    late_lists,
    part,
    edge_m,
    col_m,
    edge_mask,
    groups,
    points,
    row_taps,
    col_taps,
    images,
    mask,
    taps,
    row_m,
    values,
    upper,
    lower,
    totals,
    counts,
    small_sems,
    image_sems,
    mask_sems,
):
    visits, height, _ = images.shape
    small = [
        pltpu.make_async_copy(source, target, small_sems.at[i])
        for i, (source, target) in enumerate(
            ((groups_h, groups), (points_h, points), (row_taps_h, row_taps), (col_taps_h, col_taps))
        )
    ]

    middle = visits // 2 // UNROLL * UNROLL if visits % UNROLL == 0 else visits // 2

    def image_copy(i):
        at = pl.ds(0, middle) if i == 0 else pl.ds(middle, visits - middle)
        return pltpu.make_async_copy(images_h.at[0, at], images.at[at], image_sems.at[i])

    def mask_copy(i):
        at = pl.ds(0, middle) if i == 0 else pl.ds(middle, visits - middle)
        return pltpu.make_async_copy(mask_h.at[0, at], mask.at[at], mask_sems.at[i])

    for copy in small:
        copy.start()
    for i in range(2):
        image_copy(i).start()
        mask_copy(i).start()
    taps[...] = jnp.zeros_like(taps)
    totals[...] = jnp.zeros_like(totals)
    counts[...] = jnp.zeros_like(counts)
    row, col = square_masks()
    near = jnp.abs(row - col) <= HALF
    for copy in small:
        copy.wait()
    def build(v, slot):
        taps[slot : slot + 1, 0:TAPS] = row_taps[v]
        taps[slot + 8 : slot + 9, 0:TAPS] = col_taps[v]
        scale = points[0, groups[0, v]]
        square = around_matrix(taps[slot : slot + 1, :])
        row_m[v] = jnp.concatenate(split2(jnp.where(near, square, 0.0)), axis=1)
        far = jnp.where(near, 0.0, square)
        far = pltpu.roll(jnp.concatenate([far[:EDGE], far[height - EDGE :]], axis=0), EDGE, 1)
        edge_m[v] = jnp.concatenate(split2(far), axis=0)
        col_m[v] = col_matrix(taps[slot + 8 : slot + 9, :] * scale)

    def smear(v):
        image = images[v]
        smeared = jnp.dot(
            row_m[v], jnp.concatenate([image, image], axis=0), preferred_element_type=F32
        )
        values[v] = smeared[EDGE : height - EDGE]
        part[v, 0:EDGE] = smeared[:EDGE]
        part[v, EDGE : 2 * EDGE] = smeared[height - EDGE :]

    def convolve(v, number):
        results = [col_conv(values[v + i], col_m[v + i]) for i in range(number)]
        masks = [mask[v + i, EDGE : height - EDGE] for i in range(number)]
        hold(v, results, masks, upper, lower, totals, counts)
        for i in range(number):
            edge_mask[v + i, 0:EDGE] = mask[v + i, 0:EDGE]
            edge_mask[v + i, EDGE : 2 * EDGE] = mask[v + i, height - EDGE :]

    at_once = UNROLL if visits % UNROLL == 0 else 1
    steps = visits // at_once

    def work(step, most=None):
        convolve(step * at_once, at_once)
        for i in range(at_once):
            if most is None or most >= 1:
                smear((step + 1) * at_once + i)
        for i in range(at_once):
            if most is None or most >= 2:
                build((step + 2) * at_once + i, 16 * i)

    for step in range(min(2, steps)):
        for i in range(at_once):
            build(step * at_once + i, 16 * i)
    image_copy(0).wait()
    mask_copy(0).wait()
    for i in range(at_once):
        smear(i)
    ready = max(min(middle // at_once - 1, steps - 2), 0)

    def body(step, carry):
        work(step)
        return carry

    lax.fori_loop(0, ready, body, 0)
    image_copy(1).wait()
    mask_copy(1).wait()
    lax.fori_loop(ready, steps - 2, body, 0)
    for step in range(max(steps - 2, 0), steps):
        work(step, steps - 1 - step)
    held = (at_once, upper, lower, totals, counts)
    sort_visits(*held, 0, early_lists)
    sort_visits(*held, early_lists.shape[1], late_lists)


def at_ends(first, second):
    strip = lax.axis_index("sky")
    even = lax.rem(strip, 2) == 0
    top, bottom = strip == 0, strip == lax.axis_size("sky") - 1
    above, below = jnp.where(even, second, first), jnp.where(even, first, second)
    return (
        jnp.where(top, jnp.zeros_like(above), above),
        jnp.where(bottom, jnp.zeros_like(below), below),
    )


def edge_kernel(
    first, second, part, edge_m, col_m, edge_mask, lists, values, upper, lower, totals, counts
):
    visits, _, cols = values.shape
    for visit in range(visits):
        before, after = at_ends(first[visit], second[visit])
        window = jnp.concatenate([before, after], axis=0)
        both = jnp.dot(edge_m[visit, :, 0 : 2 * EDGE], window, preferred_element_type=F32)
        values[visit] = part[visit] + (both[: 2 * EDGE] + both[2 * EDGE :])
    at_once = UNROLL if visits % UNROLL == 0 else 1
    totals[...] = jnp.zeros_like(totals)
    counts[...] = jnp.zeros_like(counts)
    for visit in range(0, visits, at_once):
        results = [col_conv(values[visit + i], col_m[visit + i]) for i in range(at_once)]
        masks = [edge_mask[visit + i] for i in range(at_once)]
        hold(visit, results, masks, upper, lower, totals, counts)
    sort_visits(at_once, upper, lower, totals, counts, 0, lists)


def merge(mine, other, coadd, start):
    def body(step, carry):
        at = pl.ds(pl.multiple_of(step * 8, 8), 8)
        upper, lower = 0.0, 0.0
        for i in range(REJECT):
            j = REJECT - 1 - i
            upper = upper + jnp.maximum(mine[i, at, :], other[j, at, :])
            lower = lower + jnp.minimum(mine[REJECT + i, at, :], other[REJECT + j, at, :])
        total = mine[2 * REJECT, at, :] + other[2 * REJECT, at, :]
        count = mine[2 * REJECT + 1, at, :] + other[2 * REJECT + 1, at, :]
        coadd[pl.ds(pl.multiple_of(step * 8 + start, 8), 8), :] = (total - upper - lower) / (
            count - 2 * REJECT
        )
        return carry

    lax.fori_loop(0, mine.shape[1] // 8, body, 0)


def edge_merge_kernel(mine, other, coadd, send_first, send_second):
    merge(mine, other, coadd, 0)
    even = lax.rem(lax.axis_index("sky"), 2) == 0
    top, bottom = coadd[0:EDGE], coadd[EDGE : 2 * EDGE]
    send_first[...] = jnp.where(even, bottom, top).astype(BF16)
    send_second[...] = jnp.where(even, top, bottom).astype(BF16)


def lane_sums(squares):
    rows, cols = squares.shape
    part = jnp.sum(squares.reshape(rows // 8, 8, cols), axis=0)
    return sum(part[:, n * LANES : (n + 1) * LANES] for n in range(cols // LANES))


def inner_psf_kernel(
    early_mine,
    early_other,
    late_mine,
    late_other,
    edges,
    row_taps,
    col_taps,
    coadd,
    energy,
    power,
    part,
    edge_m,
    col_m,
    taps,
):
    height = coadd.shape[1]
    merge(early_mine, early_other, coadd.at[0], EDGE)
    merge(late_mine, late_other, coadd.at[0], EDGE + early_mine.shape[1])
    coadd[0, 0:EDGE] = edges[0:EDGE]
    coadd[0, height - EDGE : height] = edges[EDGE : 2 * EDGE]
    taps[...] = jnp.zeros_like(taps)
    taps[0:1, 0:TAPS] = row_taps[...]
    taps[8:9, 0:TAPS] = col_taps[...]
    row, col = square_masks()
    near = jnp.abs(row - col) <= HALF
    square = around_matrix(taps[0:1, :])
    row_h, row_l = split2(jnp.where(near, square, 0.0))
    far = jnp.where(near, 0.0, square)
    far = pltpu.roll(jnp.concatenate([far[:EDGE], far[height - EDGE :]], axis=0), EDGE, 1)
    edge_m[...] = jnp.concatenate(split2(far), axis=0)
    matrix = col_matrix(taps[8:9, :])
    col_m[...] = matrix
    high, low = split2(coadd[0])
    smeared = jnp.dot(
        jnp.concatenate([row_h, row_l], axis=1),
        jnp.concatenate([high, high], axis=0),
        preferred_element_type=F32,
    ) + jnp.dot(row_h, low, preferred_element_type=F32)
    part[0:EDGE] = smeared[:EDGE]
    part[EDGE : 2 * EDGE] = smeared[height - EDGE :]
    filtered = col_conv(smeared[EDGE : height - EDGE], matrix)
    squares = filtered * filtered
    energy[...] = squares
    power[...] = lane_sums(squares)


def edge_psf_kernel(first, second, part, edge_m, col_m, inner, inner_power, energy, power, send):
    before, after = at_ends(first[...], second[...])
    window = jnp.concatenate([before, after], axis=0)
    both = jnp.dot(edge_m[:, 0 : 2 * EDGE], window, preferred_element_type=F32)
    filtered = col_conv(part[...] + (both[: 2 * EDGE] + both[2 * EDGE :]), col_m[...])
    squares = filtered * filtered
    energy[...] = squares
    total = inner_power[...] + lane_sums(squares)
    power[...] = total
    others, rows, width = send.shape
    half = rows - EDGE - 8
    own, core = lax.axis_index("band"), lax.axis_index("exp")
    for k in range(others):
        band = lax.rem(own + k + 1, others + 1)
        lanes = pl.ds(pl.multiple_of(band * width, width), width)
        send[k, 0:EDGE] = energy[pl.ds(pl.multiple_of(core * EDGE, EDGE), EDGE), lanes]
        send[k, EDGE : EDGE + half] = inner[pl.ds(pl.multiple_of(core * half, half), half), lanes]
        for n in range(width // LANES):
            send[k, EDGE + half : rows, n * LANES : (n + 1) * LANES] = total


def final_kernel(pixels, edges, inner, *refs):
    others = (len(refs) - 2) // 2
    mine, theirs, sums, detection = refs[:others], refs[others : 2 * others], refs[-2], refs[-1]
    height, width = detection.shape
    half = inner.shape[0] // 2
    lanes = pl.ds(pl.multiple_of(lax.axis_index("band") * width, width), width)
    scales = []
    for i in range(others + 1):
        whole = jnp.sum(jnp.sum(sums[i], axis=0, keepdims=True), axis=1, keepdims=True)
        scales.append(1.0 / (whole / pixels + EPSILON))
    core = lax.axis_index("exp")
    for place, parts in ((core, mine), (1 - core, theirs)):
        for own, rows, to, start in (
            (edges, EDGE, place * (height - EDGE), 0),
            (inner, half, EDGE + place * half, EDGE),
        ):
            total = own[pl.ds(pl.multiple_of(place * rows, rows), rows), lanes] * scales[0]
            for i in range(others):
                total = total + parts[i][start : start + rows, :] * scales[i + 1]
            detection[pl.ds(pl.multiple_of(to, EDGE), rows), :] = total


def vmem(shape, dtype=F32):
    return jax.ShapeDtypeStruct(shape, dtype)


VMEM = pl.BlockSpec(memory_space=pltpu.VMEM)
SMEM = pl.BlockSpec(memory_space=pltpu.SMEM)
HBM = pl.BlockSpec(memory_space=pltpu.HBM)
PARAMS = pltpu.CompilerParams(vmem_limit_bytes=24 * MIB)


def paired(value, start):
    strips, cores = lax.axis_size("sky"), lax.axis_size("exp")
    partner = {}
    for i in range(start, strips - 1, 2):
        partner[i], partner[i + 1] = i + 1, i
    pairs = []
    for strip in range(strips):
        for core in range(cores):
            to = (partner[strip], core) if strip in partner else (strip, cores - 1 - core)
            pairs.append((strip * cores + core, to[0] * cores + to[1]))
    return lax.ppermute(value, ("sky", "exp"), pairs)


def flipped(value, axis, bits):
    return lax.ppermute(value, axis, [(i, i ^ bits) for i in range(lax.axis_size(axis))])


def turned(value, axis, step):
    size = lax.axis_size(axis)
    return lax.ppermute(value, axis, [(i, (i + step) % size) for i in range(size)])


def on_device(images, valid_mask, row_kernel, col_kernel, exp_group, zero_point, psf_row, psf_col):
    _, visits, height, cols = images.shape
    inner = height - 2 * EDGE
    bands = lax.axis_size("band")
    strips = lax.axis_size("sky")
    first, second = pl.pallas_call(
        rim_kernel,
        in_specs=[HBM],
        out_specs=[VMEM] * 2,
        out_shape=[vmem((visits, EDGE, cols), BF16)] * 2,
        scratch_shapes=[pltpu.SemaphoreType.DMA((2,))],
        compiler_params=PARAMS,
        name="rims",
    )(pltpu.with_memory_space_constraint(images, pltpu.HBM))
    first, second = paired(first, 0), paired(second, 1)

    lists = 2 * REJECT + 2
    early = inner * 5 // 8 // 8 * 8
    early_lists, late_lists, part, edge_m, col_m, edge_mask = pl.pallas_call(
        inner_kernel,
        in_specs=[HBM] * 6,
        out_specs=[VMEM] * 6,
        out_shape=[
            vmem((lists, early, cols)),
            vmem((lists, inner - early, cols)),
            vmem((visits, 2 * EDGE, cols)),
            vmem((visits, 4 * EDGE, LANES), BF16),
            vmem((visits, 2 * LANES, 2 * LANES), BF16),
            vmem((visits, 2 * EDGE, cols), jnp.int32),
        ],
        scratch_shapes=[
            pltpu.SMEM((1, visits), jnp.int32),
            pltpu.SMEM(zero_point.shape, F32),
            pltpu.VMEM((visits, 1, TAPS), F32),
            pltpu.VMEM((visits, 1, TAPS), F32),
            pltpu.VMEM((visits, height, cols), BF16),
            pltpu.VMEM((visits, height, cols), jnp.int32),
            pltpu.VMEM((16 * UNROLL, LANES), F32),
            pltpu.VMEM((visits, LANES, 2 * LANES), BF16),
            pltpu.VMEM((visits, inner, cols), F32),
            pltpu.VMEM((visits, inner, cols), F32),
            pltpu.VMEM((visits, inner, cols), F32),
            pltpu.VMEM((inner, cols), F32),
            pltpu.VMEM((inner, cols), jnp.int32),
            pltpu.SemaphoreType.DMA((4,)),
            pltpu.SemaphoreType.DMA((2,)),
            pltpu.SemaphoreType.DMA((2,)),
        ],
        compiler_params=PARAMS,
        cost_estimate=pl.CostEstimate(
            flops=visits * height * cols * 4096,
            bytes_accessed=visits * height * cols * 6,
            transcendentals=0,
        ),
        name="inner_visits",
    )(
        *(
            pltpu.with_memory_space_constraint(value, pltpu.HBM)
            for value in (
                exp_group,
                zero_point,
                images,
                valid_mask,
                row_kernel.transpose(1, 0, 2),
                col_kernel.transpose(1, 0, 2),
            )
        )
    )
    swap = [(0, 1), (1, 0)]
    held, first, second = lax.optimization_barrier((early_lists, first, second))
    early_other = lax.ppermute(held, "exp", swap)
    edge_lists = pl.pallas_call(
        edge_kernel,
        in_specs=[VMEM] * 6,
        out_specs=VMEM,
        out_shape=vmem((lists, 2 * EDGE, cols)),
        scratch_shapes=[pltpu.VMEM((visits, 2 * EDGE, cols), F32)] * 3
        + [pltpu.VMEM((2 * EDGE, cols), F32), pltpu.VMEM((2 * EDGE, cols), jnp.int32)],
        compiler_params=PARAMS,
        cost_estimate=pl.CostEstimate(
            flops=visits * height * cols * 6144, bytes_accessed=visits * cols * 256, transcendentals=0
        ),
        name="edge_visits",
    )(first, second, part, edge_m, col_m, edge_mask)
    edge_other = lax.ppermute(edge_lists, "exp", swap)

    held, _ = lax.optimization_barrier((late_lists, edge_other))
    late_other = lax.ppermute(held, "exp", swap)

    edges, send_first, send_second = pl.pallas_call(
        edge_merge_kernel,
        in_specs=[VMEM] * 2,
        out_specs=[VMEM] * 3,
        out_shape=[vmem((2 * EDGE, cols)), vmem((EDGE, cols), BF16), vmem((EDGE, cols), BF16)],
        compiler_params=PARAMS,
        name="edge_merge",
    )(edge_lists, edge_other)
    coadd_first = paired(send_first, 0)
    coadd_second = paired(send_second, 1)
    coadd_image, inner_energy, inner_power, psf_part, psf_edge_m, psf_col_m = pl.pallas_call(
        inner_psf_kernel,
        in_specs=[VMEM] * 7,
        out_specs=[VMEM] * 6,
        out_shape=[
            vmem((1, height, cols)),
            vmem((inner, cols)),
            vmem((8, LANES)),
            vmem((2 * EDGE, cols)),
            vmem((4 * EDGE, LANES), BF16),
            vmem((2 * LANES, 2 * LANES), BF16),
        ],
        scratch_shapes=[pltpu.VMEM((16, LANES), F32)],
        compiler_params=PARAMS,
        name="inner_psf",
    )(early_lists, early_other, late_lists, late_other, edges, psf_row, psf_col)

    width = cols // bands
    edge_energy, power, send = pl.pallas_call(
        edge_psf_kernel,
        in_specs=[VMEM] * 7,
        out_specs=[VMEM] * 3,
        out_shape=[
            vmem((2 * EDGE, cols)),
            vmem((8, LANES)),
            vmem((bands - 1, height // 2 + 8, width)),
        ],
        compiler_params=PARAMS,
        name="edge_psf",
    )(coadd_first, coadd_second, psf_part, psf_edge_m, psf_col_m, inner_energy, inner_power)

    mine = [turned(send[k - 1], "band", k) for k in range(1, bands)]
    held = [part[height // 2 :, :LANES] for part in mine]
    if strips == 4 and bands == 2 and lax.axis_size("exp") == 2:
        first_core = lax.axis_index("exp") == 0
        total = 0.0
        for bits in (1, 3, 2):
            pairs = []
            for strip in range(strips):
                for core in range(2):
                    for band in range(2):
                        to = (strip ^ bits, core, band ^ core)
                        pairs.append((4 * strip + 2 * core + band, 4 * to[0] + 2 * to[1] + to[2]))
            total = total + lax.ppermute(power, ("sky", "exp", "band"), pairs)
        total = total + jnp.where(first_core, power, held[0])
        theirs = [lax.ppermute(mine[0], "exp", swap)]
        total, _ = lax.optimization_barrier((total, theirs[0]))
        other = lax.ppermute(total, "exp", swap)
        sums = jnp.where(first_core, jnp.stack([total, other]), jnp.stack([other, total]))
    else:
        theirs = [lax.ppermute(part, "exp", swap) for part in mine]
        sums = lax.psum(jnp.stack([power] + held), "sky")
    pixels = height * strips * cols
    detection = pl.pallas_call(
        functools.partial(final_kernel, pixels),
        in_specs=[VMEM] * (2 * bands + 1),
        out_specs=VMEM,
        out_shape=vmem((height, width)),
        compiler_params=PARAMS,
        name="detection",
    )(edge_energy, inner_energy, *mine, *theirs, sums)
    return coadd_image, detection


def solution(mesh):
    placed = (
        P("band", "exp", ("patch", "sky"), None),
        P("band", "exp", ("patch", "sky"), None),
        P("band", "exp", None),
        P("band", "exp", None),
        P("band", "exp"),
        P("band", None),
        P("band", None),
        P("band", None),
    )
    return jax.shard_map(
        on_device,
        mesh=mesh,
        in_specs=placed,
        out_specs=(P("band", ("patch", "sky"), None), P(("patch", "sky"), "band")),
        check_vma=False,
    )
```

```python
import functools

import jax
import jax.numpy as jnp
from jax import lax
from jax.experimental import pallas as pl
from jax.experimental.pallas import tpu as pltpu
from jax.sharding import PartitionSpec as P

HALF = 15
REJECT = 4
TAPS = 31
EDGE = 16
LANES = 128
SENTINEL = 1e30
EPSILON = 1e-05
F32 = jnp.float32
BF16 = jnp.bfloat16
MIB = 1024 * 1024
UNROLL = 2


def split2(value):
    high = value.astype(BF16)
    return high, (value - high.astype(F32)).astype(BF16)


def band_rows(taps, rows):
    return pltpu.roll(
        jnp.broadcast_to(pltpu.roll(taps, 1, 1), (rows, LANES)), 0, 1, stride=1, stride_axis=0
    )


def around_matrix(taps):
    base = pltpu.roll(taps, LANES - HALF, 1)
    return pltpu.roll(jnp.broadcast_to(base, (LANES, LANES)), 0, 1, stride=1, stride_axis=0)


def square_masks():
    row = lax.broadcasted_iota(jnp.int32, (LANES, LANES), 0)
    col = lax.broadcasted_iota(jnp.int32, (LANES, LANES), 1)
    return row, col


def col_matrix(taps):
    return jnp.concatenate(split2(row_matrix(taps)), axis=0)


def row_matrix(taps):
    square = band_rows(taps, LANES)
    row, col = square_masks()
    return jnp.concatenate(
        [jnp.where(col > row, square, 0.0), jnp.where(col < row, square, 0.0)], axis=1
    )


def col_conv(value, matrix):
    rows, cols = value.shape
    tiles = cols // LANES
    turned = pltpu.roll(value, EDGE, 1)
    first = turned[:, :LANES]
    lane = lax.broadcasted_iota(jnp.int32, (rows, LANES), 1)
    wide = jnp.concatenate(
        [jnp.where(lane < EDGE, 0.0, first), turned[:, LANES:], jnp.where(lane < EDGE, first, 0.0)],
        axis=1,
    )
    parts = [
        part[:, n * LANES : (n + 2) * LANES] for part in split2(wide) for n in range(tiles)
    ]
    product = lax.dot_general(
        jnp.concatenate(parts, axis=0),
        matrix,
        (((1,), (1,)), ((), ())),
        preferred_element_type=F32,
    )

    def piece(n, side):
        return product[n * rows : (n + 1) * rows, side * LANES : (side + 1) * LANES]

    return jnp.concatenate(
        [piece(n, 0) + (piece(n, 1) + piece(tiles + n, 0)) for n in range(tiles)], axis=1
    )


def ordered(values, pairs, first, second):
    values = list(values)
    for i, j in pairs:
        values[i], values[j] = first(values[i], values[j]), second(values[i], values[j])
    return values


def foremost(groups, first, second):
    best = None
    while groups:
        group, groups = groups[0], groups[1:]
        if len(group) == 2 and groups and len(groups[0]) == 2:
            group, groups = [*group, *groups[0]], groups[1:]
            group = ordered(group, ((0, 2), (1, 3), (1, 2)), first, second)
        if best is None:
            best = group
        elif len(best) < REJECT:
            best = best + group
            pairs = [(j, j + 1) for i in range(len(best)) for j in range(len(best) - 1 - i)]
            best = ordered(best, pairs, first, second)[:REJECT]
        else:
            best = list(best)
            for i, value in enumerate(group):
                best[REJECT - 1 - i] = first(best[REJECT - 1 - i], value)
            best = ordered(best, ((0, 2), (1, 3), (0, 1), (2, 3)), first, second)
    return best


def hold(visit, results, masks, upper, lower, totals, counts):
    masks = [mask for mask in masks]
    usable = [mask == 1 for mask in masks]
    tops = [jnp.where(use, value, -SENTINEL) for use, value in zip(usable, results)]
    ends = [jnp.where(use, value, SENTINEL) for use, value in zip(usable, results)]
    if len(results) == 2:
        tops = ordered(tops, ((0, 1),), jnp.maximum, jnp.minimum)
        ends = ordered(ends, ((0, 1),), jnp.minimum, jnp.maximum)
    for i in range(len(results)):
        upper[visit + i] = tops[i]
        lower[visit + i] = ends[i]
    totals[...] += sum(jnp.where(use, value, 0.0) for use, value in zip(usable, results))
    counts[...] += sum(masks)


def sort_visits(at_once, upper, lower, totals, counts, start, lists):
    visits, _, cols = upper.shape
    rows = lists.shape[1]
    width = 2 * LANES

    def body(step, carry):
        at = pl.ds(pl.multiple_of(step * 8, 8), 8)
        source = pl.ds(pl.multiple_of(step * 8 + start, 8), 8)
        for left in range(0, cols, width):
            lanes = pl.ds(left, width)
            for place, values, first, second in (
                (0, upper, jnp.maximum, jnp.minimum),
                (REJECT, lower, jnp.minimum, jnp.maximum),
            ):
                groups = [
                    [values[v + i, source, lanes] for i in range(at_once)]
                    for v in range(0, visits, at_once)
                ]
                for i, value in enumerate(foremost(groups, first, second)):
                    lists[place + i, at, lanes] = value
            lists[2 * REJECT, at, lanes] = totals[source, lanes]
            lists[2 * REJECT + 1, at, lanes] = counts[source, lanes].astype(F32)
        return carry

    lax.fori_loop(0, rows // 8, body, 0)


def rim_kernel(images, first, second, sems):
    rows = first.shape[1]
    last = images.shape[2] - rows
    far = jnp.where(lax.rem(lax.axis_index("sky"), 2) == 0, last, 0)
    copies = [
        pltpu.make_async_copy(
            images.at[0, :, pl.ds(pl.multiple_of(start, EDGE), rows)], target, sems.at[i]
        )
        for i, (start, target) in enumerate(((far, first), (last - far, second)))
    ]
    for copy in copies:
        copy.start()
    for copy in copies:
        copy.wait()


def inner_kernel(
    groups_h,
    points_h,
    images_h,
    mask_h,
    row_taps_h,
    col_taps_h,
    early_lists,
    late_lists,
    part,
    edge_m,
    col_m,
    edge_mask,
    groups,
    points,
    row_taps,
    col_taps,
    images,
    mask,
    taps,
    row_m,
    values,
    upper,
    lower,
    totals,
    counts,
    small_sems,
    image_sems,
    mask_sems,
):
    visits, height, _ = images.shape
    small = [
        pltpu.make_async_copy(source, target, small_sems.at[i])
        for i, (source, target) in enumerate(
            ((groups_h, groups), (points_h, points), (row_taps_h, row_taps), (col_taps_h, col_taps))
        )
    ]

    middle = visits // 2 // UNROLL * UNROLL if visits % UNROLL == 0 else visits // 2

    def image_copy(i):
        at = pl.ds(0, middle) if i == 0 else pl.ds(middle, visits - middle)
        return pltpu.make_async_copy(images_h.at[0, at], images.at[at], image_sems.at[i])

    def mask_copy(i):
        at = pl.ds(0, middle) if i == 0 else pl.ds(middle, visits - middle)
        return pltpu.make_async_copy(mask_h.at[0, at], mask.at[at], mask_sems.at[i])

    for copy in small:
        copy.start()
    for i in range(2):
        image_copy(i).start()
        mask_copy(i).start()
    taps[...] = jnp.zeros_like(taps)
    totals[...] = jnp.zeros_like(totals)
    counts[...] = jnp.zeros_like(counts)
    row, col = square_masks()
    near = jnp.abs(row - col) <= HALF
    for copy in small:
        copy.wait()
    def build(v, slot):
        taps[slot : slot + 1, 0:TAPS] = row_taps[v]
        taps[slot + 8 : slot + 9, 0:TAPS] = col_taps[v]
        scale = points[0, groups[0, v]]
        square = around_matrix(taps[slot : slot + 1, :])
        row_m[v] = jnp.concatenate(split2(jnp.where(near, square, 0.0)), axis=1)
        far = jnp.where(near, 0.0, square)
        far = pltpu.roll(jnp.concatenate([far[:EDGE], far[height - EDGE :]], axis=0), EDGE, 1)
        edge_m[v] = jnp.concatenate(split2(far), axis=0)
        col_m[v] = col_matrix(taps[slot + 8 : slot + 9, :] * scale)

    def smear(v):
        image = images[v]
        smeared = jnp.dot(
            row_m[v], jnp.concatenate([image, image], axis=0), preferred_element_type=F32
        )
        values[v] = smeared[EDGE : height - EDGE]
        part[v, 0:EDGE] = smeared[:EDGE]
        part[v, EDGE : 2 * EDGE] = smeared[height - EDGE :]

    def convolve(v, number):
        results = [col_conv(values[v + i], col_m[v + i]) for i in range(number)]
        masks = [mask[v + i, EDGE : height - EDGE] for i in range(number)]
        hold(v, results, masks, upper, lower, totals, counts)
        for i in range(number):
            edge_mask[v + i, 0:EDGE] = mask[v + i, 0:EDGE]
            edge_mask[v + i, EDGE : 2 * EDGE] = mask[v + i, height - EDGE :]

    at_once = UNROLL if visits % UNROLL == 0 else 1
    steps = visits // at_once

    def work(step, most=None):
        convolve(step * at_once, at_once)
        for i in range(at_once):
            if most is None or most >= 1:
                smear((step + 1) * at_once + i)
        for i in range(at_once):
            if most is None or most >= 2:
                build((step + 2) * at_once + i, 16 * i)

    for step in range(min(2, steps)):
        for i in range(at_once):
            build(step * at_once + i, 16 * i)
    image_copy(0).wait()
    for i in range(at_once):
        smear(i)
    mask_copy(0).wait()
    ready = max(min(middle // at_once - 1, steps - 2), 0)

    def body(step, carry):
        work(step)
        return carry

    lax.fori_loop(0, ready, body, 0)
    image_copy(1).wait()
    mask_copy(1).wait()
    lax.fori_loop(ready, steps - 2, body, 0)
    for step in range(max(steps - 2, 0), steps):
        work(step, steps - 1 - step)
    held = (at_once, upper, lower, totals, counts)
    sort_visits(*held, 0, early_lists)
    sort_visits(*held, early_lists.shape[1], late_lists)


def at_ends(first, second):
    strip = lax.axis_index("sky")
    even = lax.rem(strip, 2) == 0
    top, bottom = strip == 0, strip == lax.axis_size("sky") - 1
    above, below = jnp.where(even, second, first), jnp.where(even, first, second)
    return (
        jnp.where(top, jnp.zeros_like(above), above),
        jnp.where(bottom, jnp.zeros_like(below), below),
    )


def edge_kernel(
    first, second, part, edge_m, col_m, edge_mask, lists, values, upper, lower, totals, counts
):
    visits, _, cols = values.shape
    for visit in range(visits):
        before, after = at_ends(first[visit], second[visit])
        window = jnp.concatenate([before, after], axis=0)
        both = jnp.dot(edge_m[visit, :, 0 : 2 * EDGE], window, preferred_element_type=F32)
        values[visit] = part[visit] + (both[: 2 * EDGE] + both[2 * EDGE :])
    at_once = UNROLL if visits % UNROLL == 0 else 1
    totals[...] = jnp.zeros_like(totals)
    counts[...] = jnp.zeros_like(counts)
    for visit in range(0, visits, at_once):
        results = [col_conv(values[visit + i], col_m[visit + i]) for i in range(at_once)]
        masks = [edge_mask[visit + i] for i in range(at_once)]
        hold(visit, results, masks, upper, lower, totals, counts)
    sort_visits(at_once, upper, lower, totals, counts, 0, lists)


def merge(mine, other, coadd, start):
    def body(step, carry):
        at = pl.ds(pl.multiple_of(step * 8, 8), 8)
        upper, lower = 0.0, 0.0
        for i in range(REJECT):
            j = REJECT - 1 - i
            upper = upper + jnp.maximum(mine[i, at, :], other[j, at, :])
            lower = lower + jnp.minimum(mine[REJECT + i, at, :], other[REJECT + j, at, :])
        total = mine[2 * REJECT, at, :] + other[2 * REJECT, at, :]
        count = mine[2 * REJECT + 1, at, :] + other[2 * REJECT + 1, at, :]
        coadd[pl.ds(pl.multiple_of(step * 8 + start, 8), 8), :] = (total - upper - lower) / (
            count - 2 * REJECT
        )
        return carry

    lax.fori_loop(0, mine.shape[1] // 8, body, 0)


def edge_merge_kernel(mine, other, coadd, send_first, send_second):
    merge(mine, other, coadd, 0)
    even = lax.rem(lax.axis_index("sky"), 2) == 0
    top, bottom = coadd[0:EDGE], coadd[EDGE : 2 * EDGE]
    send_first[...] = jnp.where(even, bottom, top).astype(BF16)
    send_second[...] = jnp.where(even, top, bottom).astype(BF16)


def lane_sums(squares):
    rows, cols = squares.shape
    part = jnp.sum(squares.reshape(rows // 8, 8, cols), axis=0)
    return sum(part[:, n * LANES : (n + 1) * LANES] for n in range(cols // LANES))


def inner_psf_kernel(
    early_mine,
    early_other,
    late_mine,
    late_other,
    edges,
    row_taps,
    col_taps,
    coadd,
    energy,
    power,
    part,
    edge_m,
    col_m,
    taps,
):
    height = coadd.shape[1]
    merge(early_mine, early_other, coadd.at[0], EDGE)
    merge(late_mine, late_other, coadd.at[0], EDGE + early_mine.shape[1])
    coadd[0, 0:EDGE] = edges[0:EDGE]
    coadd[0, height - EDGE : height] = edges[EDGE : 2 * EDGE]
    taps[...] = jnp.zeros_like(taps)
    taps[0:1, 0:TAPS] = row_taps[...]
    taps[8:9, 0:TAPS] = col_taps[...]
    row, col = square_masks()
    near = jnp.abs(row - col) <= HALF
    square = around_matrix(taps[0:1, :])
    row_h, row_l = split2(jnp.where(near, square, 0.0))
    far = jnp.where(near, 0.0, square)
    far = pltpu.roll(jnp.concatenate([far[:EDGE], far[height - EDGE :]], axis=0), EDGE, 1)
    edge_m[...] = jnp.concatenate(split2(far), axis=0)
    matrix = col_matrix(taps[8:9, :])
    col_m[...] = matrix
    high, low = split2(coadd[0])
    smeared = jnp.dot(
        jnp.concatenate([row_h, row_l], axis=1),
        jnp.concatenate([high, high], axis=0),
        preferred_element_type=F32,
    ) + jnp.dot(row_h, low, preferred_element_type=F32)
    part[0:EDGE] = smeared[:EDGE]
    part[EDGE : 2 * EDGE] = smeared[height - EDGE :]
    filtered = col_conv(smeared[EDGE : height - EDGE], matrix)
    squares = filtered * filtered
    energy[...] = squares
    power[...] = lane_sums(squares)


def edge_psf_kernel(first, second, part, edge_m, col_m, inner, inner_power, energy, power, send):
    before, after = at_ends(first[...], second[...])
    window = jnp.concatenate([before, after], axis=0)
    both = jnp.dot(edge_m[:, 0 : 2 * EDGE], window, preferred_element_type=F32)
    filtered = col_conv(part[...] + (both[: 2 * EDGE] + both[2 * EDGE :]), col_m[...])
    squares = filtered * filtered
    energy[...] = squares
    total = inner_power[...] + lane_sums(squares)
    power[...] = total
    others, rows, width = send.shape
    half = rows - EDGE - 8
    own, core = lax.axis_index("band"), lax.axis_index("exp")
    for k in range(others):
        band = lax.rem(own + k + 1, others + 1)
        lanes = pl.ds(pl.multiple_of(band * width, width), width)
        send[k, 0:EDGE] = energy[pl.ds(pl.multiple_of(core * EDGE, EDGE), EDGE), lanes]
        send[k, EDGE : EDGE + half] = inner[pl.ds(pl.multiple_of(core * half, half), half), lanes]
        for n in range(width // LANES):
            send[k, EDGE + half : rows, n * LANES : (n + 1) * LANES] = total


def final_kernel(pixels, edges, inner, *refs):
    others = (len(refs) - 2) // 2
    mine, theirs, sums, detection = refs[:others], refs[others : 2 * others], refs[-2], refs[-1]
    height, width = detection.shape
    half = inner.shape[0] // 2
    lanes = pl.ds(pl.multiple_of(lax.axis_index("band") * width, width), width)
    scales = []
    for i in range(others + 1):
        whole = jnp.sum(jnp.sum(sums[i], axis=0, keepdims=True), axis=1, keepdims=True)
        scales.append(1.0 / (whole / pixels + EPSILON))
    core = lax.axis_index("exp")
    for place, parts in ((core, mine), (1 - core, theirs)):
        for own, rows, to, start in (
            (edges, EDGE, place * (height - EDGE), 0),
            (inner, half, EDGE + place * half, EDGE),
        ):
            total = own[pl.ds(pl.multiple_of(place * rows, rows), rows), lanes] * scales[0]
            for i in range(others):
                total = total + parts[i][start : start + rows, :] * scales[i + 1]
            detection[pl.ds(pl.multiple_of(to, EDGE), rows), :] = total


def vmem(shape, dtype=F32):
    return jax.ShapeDtypeStruct(shape, dtype)


VMEM = pl.BlockSpec(memory_space=pltpu.VMEM)
SMEM = pl.BlockSpec(memory_space=pltpu.SMEM)
HBM = pl.BlockSpec(memory_space=pltpu.HBM)
PARAMS = pltpu.CompilerParams(vmem_limit_bytes=24 * MIB)


def paired(value, start):
    strips, cores = lax.axis_size("sky"), lax.axis_size("exp")
    partner = {}
    for i in range(start, strips - 1, 2):
        partner[i], partner[i + 1] = i + 1, i
    pairs = []
    for strip in range(strips):
        for core in range(cores):
            to = (partner[strip], core) if strip in partner else (strip, cores - 1 - core)
            pairs.append((strip * cores + core, to[0] * cores + to[1]))
    return lax.ppermute(value, ("sky", "exp"), pairs)


def flipped(value, axis, bits):
    return lax.ppermute(value, axis, [(i, i ^ bits) for i in range(lax.axis_size(axis))])


def turned(value, axis, step):
    size = lax.axis_size(axis)
    return lax.ppermute(value, axis, [(i, (i + step) % size) for i in range(size)])


def on_device(images, valid_mask, row_kernel, col_kernel, exp_group, zero_point, psf_row, psf_col):
    _, visits, height, cols = images.shape
    inner = height - 2 * EDGE
    bands = lax.axis_size("band")
    strips = lax.axis_size("sky")
    first, second = pl.pallas_call(
        rim_kernel,
        in_specs=[HBM],
        out_specs=[VMEM] * 2,
        out_shape=[vmem((visits, EDGE, cols), BF16)] * 2,
        scratch_shapes=[pltpu.SemaphoreType.DMA((2,))],
        compiler_params=PARAMS,
        name="rims",
    )(pltpu.with_memory_space_constraint(images, pltpu.HBM))
    first, second = paired(first, 0), paired(second, 1)

    lists = 2 * REJECT + 2
    early = inner * 5 // 8 // 8 * 8
    early_lists, late_lists, part, edge_m, col_m, edge_mask = pl.pallas_call(
        inner_kernel,
        in_specs=[HBM] * 6,
        out_specs=[VMEM] * 6,
        out_shape=[
            vmem((lists, early, cols)),
            vmem((lists, inner - early, cols)),
            vmem((visits, 2 * EDGE, cols)),
            vmem((visits, 4 * EDGE, LANES), BF16),
            vmem((visits, 2 * LANES, 2 * LANES), BF16),
            vmem((visits, 2 * EDGE, cols), jnp.int32),
        ],
        scratch_shapes=[
            pltpu.SMEM((1, visits), jnp.int32),
            pltpu.SMEM(zero_point.shape, F32),
            pltpu.VMEM((visits, 1, TAPS), F32),
            pltpu.VMEM((visits, 1, TAPS), F32),
            pltpu.VMEM((visits, height, cols), BF16),
            pltpu.VMEM((visits, height, cols), jnp.int32),
            pltpu.VMEM((16 * UNROLL, LANES), F32),
            pltpu.VMEM((visits, LANES, 2 * LANES), BF16),
            pltpu.VMEM((visits, inner, cols), F32),
            pltpu.VMEM((visits, inner, cols), F32),
            pltpu.VMEM((visits, inner, cols), F32),
            pltpu.VMEM((inner, cols), F32),
            pltpu.VMEM((inner, cols), jnp.int32),
            pltpu.SemaphoreType.DMA((4,)),
            pltpu.SemaphoreType.DMA((2,)),
            pltpu.SemaphoreType.DMA((2,)),
        ],
        compiler_params=PARAMS,
        cost_estimate=pl.CostEstimate(
            flops=visits * height * cols * 4096,
            bytes_accessed=visits * height * cols * 6,
            transcendentals=0,
        ),
        name="inner_visits",
    )(
        *(
            pltpu.with_memory_space_constraint(value, pltpu.HBM)
            for value in (
                exp_group,
                zero_point,
                images,
                valid_mask,
                row_kernel.transpose(1, 0, 2),
                col_kernel.transpose(1, 0, 2),
            )
        )
    )
    swap = [(0, 1), (1, 0)]
    held, first, second = lax.optimization_barrier((early_lists, first, second))
    early_other = lax.ppermute(held, "exp", swap)
    edge_lists = pl.pallas_call(
        edge_kernel,
        in_specs=[VMEM] * 6,
        out_specs=VMEM,
        out_shape=vmem((lists, 2 * EDGE, cols)),
        scratch_shapes=[pltpu.VMEM((visits, 2 * EDGE, cols), F32)] * 3
        + [pltpu.VMEM((2 * EDGE, cols), F32), pltpu.VMEM((2 * EDGE, cols), jnp.int32)],
        compiler_params=PARAMS,
        cost_estimate=pl.CostEstimate(
            flops=visits * height * cols * 6144, bytes_accessed=visits * cols * 256, transcendentals=0
        ),
        name="edge_visits",
    )(first, second, part, edge_m, col_m, edge_mask)
    edge_other = lax.ppermute(edge_lists, "exp", swap)

    held, _ = lax.optimization_barrier((late_lists, edge_other))
    late_other = lax.ppermute(held, "exp", swap)

    edges, send_first, send_second = pl.pallas_call(
        edge_merge_kernel,
        in_specs=[VMEM] * 2,
        out_specs=[VMEM] * 3,
        out_shape=[vmem((2 * EDGE, cols)), vmem((EDGE, cols), BF16), vmem((EDGE, cols), BF16)],
        compiler_params=PARAMS,
        name="edge_merge",
    )(edge_lists, edge_other)
    coadd_first = paired(send_first, 0)
    coadd_second = paired(send_second, 1)
    coadd_image, inner_energy, inner_power, psf_part, psf_edge_m, psf_col_m = pl.pallas_call(
        inner_psf_kernel,
        in_specs=[VMEM] * 7,
        out_specs=[VMEM] * 6,
        out_shape=[
            vmem((1, height, cols)),
            vmem((inner, cols)),
            vmem((8, LANES)),
            vmem((2 * EDGE, cols)),
            vmem((4 * EDGE, LANES), BF16),
            vmem((2 * LANES, 2 * LANES), BF16),
        ],
        scratch_shapes=[pltpu.VMEM((16, LANES), F32)],
        compiler_params=PARAMS,
        name="inner_psf",
    )(early_lists, early_other, late_lists, late_other, edges, psf_row, psf_col)

    width = cols // bands
    edge_energy, power, send = pl.pallas_call(
        edge_psf_kernel,
        in_specs=[VMEM] * 7,
        out_specs=[VMEM] * 3,
        out_shape=[
            vmem((2 * EDGE, cols)),
            vmem((8, LANES)),
            vmem((bands - 1, height // 2 + 8, width)),
        ],
        compiler_params=PARAMS,
        name="edge_psf",
    )(coadd_first, coadd_second, psf_part, psf_edge_m, psf_col_m, inner_energy, inner_power)

    mine = [turned(send[k - 1], "band", k) for k in range(1, bands)]
    held = [part[height // 2 :, :LANES] for part in mine]
    if strips == 4 and bands == 2 and lax.axis_size("exp") == 2:
        first_core = lax.axis_index("exp") == 0
        total = 0.0
        for bits in (1, 3, 2):
            pairs = []
            for strip in range(strips):
                for core in range(2):
                    for band in range(2):
                        to = (strip ^ bits, core, band ^ core)
                        pairs.append((4 * strip + 2 * core + band, 4 * to[0] + 2 * to[1] + to[2]))
            total = total + lax.ppermute(power, ("sky", "exp", "band"), pairs)
        total = total + jnp.where(first_core, power, held[0])
        theirs = [lax.ppermute(mine[0], "exp", swap)]
        total, _ = lax.optimization_barrier((total, theirs[0]))
        other = lax.ppermute(total, "exp", swap)
        sums = jnp.where(first_core, jnp.stack([total, other]), jnp.stack([other, total]))
    else:
        theirs = [lax.ppermute(part, "exp", swap) for part in mine]
        sums = lax.psum(jnp.stack([power] + held), "sky")
    pixels = height * strips * cols
    detection = pl.pallas_call(
        functools.partial(final_kernel, pixels),
        in_specs=[VMEM] * (2 * bands + 1),
        out_specs=VMEM,
        out_shape=vmem((height, width)),
        compiler_params=PARAMS,
        name="detection",
    )(edge_energy, inner_energy, *mine, *theirs, sums)
    return coadd_image, detection


def solution(mesh):
    placed = (
        P("band", "exp", ("patch", "sky"), None),
        P("band", "exp", ("patch", "sky"), None),
        P("band", "exp", None),
        P("band", "exp", None),
        P("band", "exp"),
        P("band", None),
        P("band", None),
        P("band", None),
    )
    return jax.shard_map(
        on_device,
        mesh=mesh,
        in_specs=placed,
        out_specs=(P("band", ("patch", "sky"), None), P(("patch", "sky"), "band")),
        check_vma=False,
    )
```
